256 devices in a mesh: sub: 64 (over z, x, core), loc: 4 (over y).
Axes of the slice: x: 4, y: 4, z: 8, core: 2. Of those that a mesh axis runs over, the one named last changes fastest.
Arguments:
- interface_load: float32 [256, 16, 2048], P(('sub', 'loc')), may hold values from -60 to 60
- flexibility: bfloat16 [256, 2048, 2048], P(('sub', 'loc')), may hold values from -2 to 4, as said below
- corner_coupling: float32 [256, 24, 2048], P(('sub', 'loc')), may hold values from -0.125 to 0.125
- coarse_factor: float32 [2048, 2048], P('loc'), may hold values from -3 to 3, as said below
- face_slots: int32 [256, 4, 4], P(('sub', 'loc')), may hold values from -1 to 15, as said below
- corner_map: int32 [256, 24], P(('sub', 'loc')), may hold values from 0 to 2047, as said below
Outputs:
- multipliers: float32 [256, 16, 2048], P(('sub', 'loc'))
- residual: float32 [256, 16, 2048], P(('sub', 'loc'))
The draws below stay inside these ranges and needn't reach their ends.
Inputs may be any that keep to these rules, and one draw needn't show every extreme that they name: `face_slots`: slots of a face are filled from slot 0; slot c of face d of s is filled exactly when slot c of face d XOR 1 of the neighbour of face d is; a block stands in at most one slot of its subdomain; faces toward no subdomain of the grid are empty (-1); some face has all 4 slots filled. `corner_map`: the 24 entries of a subdomain are distinct. `flexibility`: each subdomain's matrix is symmetric positive definite. `coarse_factor`: lower triangular with a positive diagonal.
All inputs are finite; a program needn't handle non-finite values.
Results may differ from the reference program's by a relative error of at most 0.0038.
Values sent between devices are 32-bit elements; how exact they have to be, the bound alone decides.
No kernel may reach another device: no remote copies, remote signals or barrier semaphores. Data moves between devices by JAX's collectives and lax.ppermute only.
A program may use at most 128 MiB of HBM per device.

```python
import math
import jax
import jax.numpy as jnp
from jax import lax

INTERFACE = 2048
BLOCK_ROWS = 128
FACE_MOST = 4
LOAD_CASES = 16
CORNERS = 24
ITERATIONS = 2
GRID_ROWS = 64
GRID_COLS = 4
DOMAINS = 256
BLOCKS = 16
COARSE = 2048


def draw_face_slots(key, part):
    key = jax.random.fold_in(key, 11)
    sub_key, loc_key, perm_key = jax.random.split(key, 3)
    down_counts = jax.random.randint(sub_key, (GRID_ROWS - 1, GRID_COLS), 1, FACE_MOST + 1).astype(jnp.int32)
    down_counts = down_counts.at[0, 0].set(FACE_MOST)
    across = jax.random.randint(loc_key, (GRID_ROWS, GRID_COLS - 1), 1, FACE_MOST + 1).astype(jnp.int32)
    zero_row = jnp.zeros((1, GRID_COLS), jnp.int32)
    zero_col = jnp.zeros((GRID_ROWS, 1), jnp.int32)
    counts = jnp.stack([jnp.concatenate([zero_row, down_counts], axis=0), jnp.concatenate([down_counts, zero_row], axis=0), jnp.concatenate([zero_col, across], axis=1), jnp.concatenate([across, zero_col], axis=1)], axis=-1).reshape(DOMAINS, 4)
    row_keys = jax.random.split(perm_key, DOMAINS)
    orders = jax.vmap(lambda row_key: jax.random.permutation(row_key, BLOCKS))(row_keys).astype(jnp.int32)
    lead_row = orders[0]
    lead_spot = jnp.argmax(lead_row == BLOCKS - 1)
    orders = orders.at[0].set(jnp.roll(lead_row, -lead_spot))
    starts = jnp.cumsum(counts, axis=1) - counts
    slot_index = jnp.arange(FACE_MOST, dtype=jnp.int32)
    position = jnp.clip(starts[:, :, None] + slot_index[None, None, :], 0, BLOCKS - 1)
    filled = slot_index[None, None, :] < counts[:, :, None]
    domain_ids = jnp.arange(DOMAINS, dtype=jnp.int32)
    picked = orders[domain_ids[:, None, None], position]
    return jnp.where(filled, picked, -1).astype(jnp.int32)


def draw_corner_map(key, part):
    key = jax.random.fold_in(key, 23)
    row_keys = jax.random.split(key, DOMAINS)
    orders = jax.vmap(lambda row_key: jax.random.permutation(row_key, COARSE))(row_keys).astype(jnp.int32)
    lead_row = orders[0]
    orders = orders.at[0].set(jnp.roll(lead_row, -jnp.argmax(lead_row == COARSE - 1)))
    next_row = orders[1]
    orders = orders.at[1].set(jnp.roll(next_row, -jnp.argmax(next_row == 0)))
    return orders[:, :CORNERS].astype(jnp.int32)


def draw_flexibility(key, part):
    key = jax.random.fold_in(key, 37)

    def single(domain_index):
        sub_key = jax.random.fold_in(key, domain_index)
        key_noise, key_diag = jax.random.split(sub_key, 2)
        gauss_part = jnp.clip(jax.random.normal(key_noise, (INTERFACE, INTERFACE), jnp.float32), -6.0, 6.0)
        diagonal = 0.9 + 0.8 * jax.random.uniform(key_diag, (INTERFACE,), jnp.float32)
        matrix = (gauss_part + gauss_part.T) * (0.2 / math.sqrt(INTERFACE)) + jnp.diag(diagonal)
        return matrix.astype(jnp.bfloat16)
    return lax.map(single, jnp.arange(DOMAINS, dtype=jnp.int32))


def draw_coarse_factor(key, part):
    key = jax.random.fold_in(key, 41)
    key_noise, key_diag = jax.random.split(key, 2)
    row_index = jnp.arange(COARSE, dtype=jnp.int32)[:, None]
    col_index = jnp.arange(COARSE, dtype=jnp.int32)[None, :]
    gauss_part = jnp.clip(jax.random.normal(key_noise, (COARSE, COARSE), jnp.float32), -6.0, 6.0)
    below = gauss_part * (0.35 / jnp.sqrt(jnp.maximum(row_index, 1).astype(jnp.float32)))
    diagonal = 0.7 + 0.6 * jax.random.uniform(key_diag, (COARSE, 1), jnp.float32)
    lower = jnp.where(col_index < row_index, below, jnp.where(col_index == row_index, diagonal, 0.0))
    return lower.astype(jnp.float32)


def draw_interface_load(key, part):
    key = jax.random.fold_in(key, 53)
    key_base, key_row, key_col = jax.random.split(key, 3)
    position = jnp.arange(DOMAINS, dtype=jnp.float32) / max(DOMAINS - 1, 1)
    shape = (DOMAINS, LOAD_CASES, INTERFACE)
    pattern = jnp.clip(jax.random.normal(key_base, shape, jnp.float32), -6.0, 6.0)
    growth = 3.0 ** position
    row_scale = jnp.exp(jax.random.uniform(key_row, (DOMAINS, LOAD_CASES, 1), jnp.float32, -1.2237754, 0.0))
    column = jnp.exp(jax.random.uniform(key_col, (1, 1, INTERFACE), jnp.float32, -0.4, 0.4))
    return (pattern * growth[:, None, None] * row_scale * column).astype(jnp.float32)


def block_scale(key, extent, cuts, smallest, top_value):
    factor_of = 1.0
    for dim, shards_of in cuts:
        heights = jax.random.uniform(jax.random.fold_in(jax.random.fold_in(key, 6), dim), (shards_of,), jnp.float32, smallest / len(cuts), top_value / len(cuts))
        factor_of = factor_of * jnp.repeat(jnp.exp(heights), extent[dim] // shards_of).reshape((-1,) + (1,) * (len(extent) - 1 - dim))
    return factor_of


def centred(stream_key, shape, scale, most, shards=(), held_as=jnp.bfloat16):
    values = scale * jax.random.normal(stream_key, shape, jnp.float32)
    if shards:
        values = values * block_scale(stream_key, shape, shards, -0.22, 0.18)
    return jnp.clip(values, -most, most).astype(held_as)


def setup_inputs(seed: int = 0) -> dict:
    streams_of = jax.random.split(jax.random.key(seed), 7)
    interface_load = draw_interface_load(jax.random.fold_in(streams_of[6], 71), 0)
    flexibility = draw_flexibility(jax.random.fold_in(streams_of[6], 71), 0)
    corner_coupling = centred(streams_of[2], (DOMAINS, CORNERS, INTERFACE), INTERFACE ** -0.5, 0.125, ((0, 256),), jnp.float32)
    coarse_factor = draw_coarse_factor(jax.random.fold_in(streams_of[6], 71), 0)
    face_slots = draw_face_slots(jax.random.fold_in(streams_of[6], 71), 0)
    corner_map = draw_corner_map(jax.random.fold_in(streams_of[6], 71), 0)
    return {"interface_load": interface_load, "flexibility": flexibility, "corner_coupling": corner_coupling, "coarse_factor": coarse_factor, "face_slots": face_slots, "corner_map": corner_map}


def jump_field(values, face_slots):
    blocked = values.reshape(DOMAINS, LOAD_CASES, BLOCKS, BLOCK_ROWS)
    domain_ids = jnp.arange(DOMAINS, dtype=jnp.int32)
    grid_row = domain_ids // GRID_COLS
    grid_col = domain_ids % GRID_COLS
    neighbour = jnp.stack([domain_ids - GRID_COLS, domain_ids + GRID_COLS, domain_ids - 1, domain_ids + 1], axis=1)
    inside = jnp.stack([grid_row > 0, grid_row < GRID_ROWS - 1, grid_col > 0, grid_col < GRID_COLS - 1], axis=1)
    neighbour = jnp.where(inside, neighbour, 0).astype(jnp.int32)
    opposite = jnp.array([1, 0, 3, 2], dtype=jnp.int32)
    partner_blocks = face_slots[neighbour, opposite[None, :], :]
    filled = inside[:, :, None] & (partner_blocks >= 0) & (face_slots >= 0)
    received = blocked[neighbour[:, :, None], :, jnp.clip(partner_blocks, 0, BLOCKS - 1)]
    received = jnp.where(filled[:, :, :, None, None], received, jnp.zeros_like(received))
    slot_table = (face_slots[:, :, :, None] == jnp.arange(BLOCKS, dtype=jnp.int32)).astype(jnp.float32)
    partner = jnp.einsum("sfcb,sfckx->skbx", slot_table, received, precision=lax.Precision.HIGHEST)
    return (blocked - partner).reshape(DOMAINS, LOAD_CASES, INTERFACE)


def block_weight(face_slots):
    slot_table = (face_slots[:, :, :, None] == jnp.arange(BLOCKS, dtype=jnp.int32)).astype(jnp.float32)
    paired = jnp.sum(slot_table, axis=(1, 2)) > 0.5
    weight = jnp.where(paired, 0.5, 1.0).astype(jnp.float32)
    return jnp.repeat(weight, BLOCK_ROWS, axis=1)


def weighted_dot(left_part, right_part, dof_weight):
    return jnp.sum(left_part * right_part * dof_weight[:, None, :], axis=(0, 2))


def local_product(operands):
    return jnp.dot(operands[0], operands[1], preferred_element_type=jnp.float32)


def apply_operator(direction, flexibility, corner_coupling, coarse_factor, face_slots, corner_map):
    highest = lax.Precision.HIGHEST
    rounded = direction.astype(jnp.bfloat16)
    local_part = lax.map(local_product, (rounded, flexibility))
    partial_value = jnp.einsum("skx,scx->skc", direction, corner_coupling, precision=highest)
    coarse_rhs = jnp.zeros((LOAD_CASES, COARSE), jnp.float32)
    coarse_rhs = coarse_rhs.at[:, corner_map.reshape(-1)].add(
        jnp.transpose(partial_value, (1, 0, 2)).reshape(LOAD_CASES, DOMAINS * CORNERS))
    coarse_mid = jnp.dot(coarse_rhs, coarse_factor.T, precision=highest)
    coarse_sol = jnp.dot(coarse_mid, coarse_factor, precision=highest)
    picked = coarse_sol[:, corner_map]
    spread = jnp.einsum("ksc,scx->skx", picked, corner_coupling, precision=highest)
    return jump_field(local_part + spread, face_slots)


def reference(interface_load, flexibility, corner_coupling, coarse_factor, face_slots, corner_map):
    dof_weight = block_weight(face_slots)
    driven = jump_field(interface_load, face_slots)
    multipliers = jnp.zeros_like(driven)
    residual = driven
    direction = driven
    norm_now = weighted_dot(residual, residual, dof_weight)
    for iteration in range(ITERATIONS):
        mapped = apply_operator(direction, flexibility, corner_coupling, coarse_factor, face_slots, corner_map)
        step_size = norm_now / weighted_dot(direction, mapped, dof_weight)
        multipliers = multipliers + step_size[None, :, None] * direction
        residual = residual - step_size[None, :, None] * mapped
        fresh_norm = weighted_dot(residual, residual, dof_weight)
        direction = residual + (fresh_norm / norm_now)[None, :, None] * direction
        norm_now = fresh_norm
    return multipliers, residual
```

```python
import functools

import jax
import jax.numpy as jnp
from jax import lax
from jax.experimental import pallas as pl
from jax.experimental.pallas import tpu as pltpu
from jax.sharding import Mesh, PartitionSpec as P

BW = 128
LANES = 32
NORM, CROSS, SQUARE, LOCAL = 24, 25, 26, 27
RADIX = 256
F32, BF16 = jnp.float32, jnp.bfloat16
ALL = ("z", "x", "c", "y")
SUB = ("z", "x", "c")

NN = (((1,), (0,)), ((), ()))
NT = (((1,), (1,)), ((), ()))

VMEM = pl.BlockSpec(memory_space=pltpu.VMEM)
SMEM = pl.BlockSpec(memory_space=pltpu.SMEM)


def params(mib):
    return pltpu.CompilerParams(vmem_limit_bytes=mib * 1024 * 1024)


def split(x):
    hi = x.astype(BF16)
    return hi, (x - hi.astype(F32)).astype(BF16)


def dot(a, b, dims):
    return lax.dot_general(a, b, dims, preferred_element_type=F32)


def dot3(a, b_hi, b_lo, dims):
    rows = a.shape[0]
    a_hi, a_lo = split(a)
    both = dot(jnp.concatenate([a_hi, a_lo], axis=0), b_hi, dims)
    return both[:rows] + both[rows:] + dot(a_hi, b_lo, dims)


def block_at(b):
    return pl.ds(pl.multiple_of(jnp.maximum(b, 0) * BW, BW), BW)


def subtract_faces(ref, slots, incoming):
    for f in range(4):
        for c in range(4):
            b = slots[f, c]
            at = block_at(b)
            held = ref[:, at]
            got = incoming[f][0:16, c * BW : (c + 1) * BW]
            ref[:, at] = jnp.where(b >= 0, held - got, held)


def pack_faces(values, slots, outs, row0):
    rows = values.shape[0]
    for f in range(4):
        for c in range(4):
            outs[f][row0 : row0 + rows, c * BW : (c + 1) * BW] = values[:, block_at(slots[f, c])]


def lane_sum(x):
    return jnp.sum(x, axis=1, keepdims=True)


def place(lane, y, slot, column):
    return jnp.where(lane == y * LANES + slot, column, 0.0)


def first_pack(slots, corners, y_ref, load, o0, o1, o2, o3, cm_row):
    pack_faces(load, slots, (o0, o1, o2, o3), 0)
    lane = lax.broadcasted_iota(jnp.int32, (8, BW), 1)
    base = y_ref[0] * LANES
    row = jnp.zeros((8, BW), jnp.int32)
    for j in range(corners.shape[1]):
        row = jnp.where(lane == base + j, corners[0, j], row)
    row = row.astype(F32)
    cm_row[...] = row
    for o in (o0, o1):
        o[16:24, 0:BW] = row
        o[16:24, BW:] = jnp.zeros((8, 3 * BW), F32)


def prepare(slots, y_ref, coupling, factor, bx_hi, bx_lo, weight, f_hi, f_lo, bx):
    bx[...] = jnp.zeros_like(bx)
    bx[pl.ds(pl.multiple_of(y_ref[0] * LANES, LANES), 24), :] = coupling[...]
    hi, lo = split(bx[...])
    bx_hi[...] = hi
    bx_lo[...] = lo
    weight[...] = jnp.ones_like(weight)
    for f in range(4):
        for c in range(4):
            b = slots[f, c]
            at = block_at(b)
            weight[:, at] = jnp.where(b >= 0, jnp.full((8, BW), 0.5, F32), weight[:, at])
    hi, lo = split(factor[...])
    f_hi[...] = hi
    f_lo[...] = lo


def first_vector(slots, y_ref, load, i0, i1, i2, i3, bx_hi, bx_lo, weight, cm_row, v0, pay):
    v0[...] = load[...]
    subtract_faces(v0, slots, (i0, i1, i2, i3))
    v = v0[...]
    norm = lane_sum(v * v * weight[0:1, :])
    lane = lax.broadcasted_iota(jnp.int32, (16, BW), 1)
    pay[0:16, :] = dot3(v, bx_hi[...], bx_lo[...], NT) + place(lane, y_ref[0], NORM, norm)
    row = lax.broadcasted_iota(jnp.int32, (8, BW), 0)
    own, up, down = (cm_row[0:1, :], i0[16:17, 0:BW], i1[16:17, 0:BW])
    pay[16:24, :] = jnp.where(
        row == 0, own, jnp.where(row == 1, up, jnp.where(row == 2, down, 0.0))
    )


def local_product(first, slots, y_ref, v, mat, *rest):
    if first:
        coupling, z, o0, o1, o2, o3, pieces = rest
    else:
        z, o0, o1, o2, o3, dot_out, pieces = rest
    step = pl.program_id(0)
    width = mat.shape[1]

    @pl.when(step == 0)
    def _():
        hi, lo = split(v[...])
        pieces[0:16, :] = hi
        pieces[16:32, :] = lo

    both = dot(pieces[...], mat[...], NN)
    z[:, pl.ds(pl.multiple_of(step * width, width), width)] = both[:16] + both[16:]

    @pl.when(step == pl.num_programs(0) - 1)
    def _():
        pack_faces(z, slots, (o0, o1, o2, o3), 0)
        if first:
            pack_faces(coupling, slots, (o0, o1, o2, o3), 16)
        else:
            lane = lax.broadcasted_iota(jnp.int32, (16, BW), 1)
            dot_out[...] = place(lane, y_ref[0], LOCAL, lane_sum(v[...] * z[...]))


def jumped_coupling(slots, y_ref, coupling, i0, i1, i2, i3, b_hi, b_lo, full):
    y = y_ref[0]
    full[...] = jnp.zeros_like(full)

    def rows(group, col):
        return pl.ds(pl.multiple_of(group * BW + col * LANES, LANES), 24)

    full[rows(0, y), :] = coupling[...]
    places = (rows(1, y), rows(2, y), rows(0, jnp.maximum(y - 1, 0)), rows(0, jnp.minimum(y + 1, 3)))
    for f, got in enumerate((i0, i1, i2, i3)):
        for c in range(4):
            b = slots[f, c]
            at = block_at(b)
            held = full[places[f], at]
            full[places[f], at] = jnp.where(b >= 0, -got[16:40, c * BW : (c + 1) * BW], held)
    hi, lo = split(full[...])
    b_hi[...] = hi
    b_lo[...] = lo


def picked_columns(pay, f_hi, f_lo, c_hi, c_lo):
    dofs = f_hi.shape[1]
    wanted = jnp.concatenate([pay[16:17, :], pay[17:18, :], pay[18:19, :]], axis=1)
    row = lax.broadcasted_iota(jnp.int32, (dofs, 3 * BW), 0)
    hot = (row == wanted.astype(jnp.int32)).astype(F32).astype(BF16)
    c_hi[...] = dot(f_hi[...], hot, NN).astype(BF16)
    c_lo[...] = dot(f_lo[...], hot, NN).astype(BF16)


def coarse(final, y_ref, ta, tb, ma, mb, f_hi, f_lo, c_hi, c_lo, part, scal, spread_rows, hot):
    groups = ta.shape[0]
    digits = f_hi.shape[1] // RADIX
    half = digits * 16
    lane = lax.broadcasted_iota(jnp.int32, (16, BW), 1)
    slot = lane % LANES
    low = lax.broadcasted_iota(jnp.int32, (RADIX, BW), 0)
    total = jnp.zeros((16, BW), F32)
    for n, (t, m) in enumerate(((ta, ma), (tb, mb))):

        def body(j, acc):
            terms = t[j, 0:16, :]
            dof = m[j, 16:17, :].astype(jnp.int32)
            top = jnp.where(slot < 24, jnp.broadcast_to(dof // RADIX, (16, BW)), -1)
            hi = terms.astype(BF16).astype(F32)
            lo = terms - hi
            at = pl.ds(pl.multiple_of((n * groups + j) * BW, BW), BW)
            for d in range(digits):
                mine = top == d
                spread_rows[d * 16 : d * 16 + 16, at] = jnp.where(mine, hi, 0.0).astype(BF16)
                spread_rows[half + d * 16 : half + d * 16 + 16, at] = jnp.where(
                    mine, lo, 0.0
                ).astype(BF16)
            hot[:, at] = (low == dof % RADIX).astype(F32).astype(BF16)
            return acc + terms

        total = lax.fori_loop(0, groups, body, total, unroll=4)
    sums = dot(spread_rows[...], hot[...], NT)
    sums = sums[:half] + sums[half:]
    rhs = jnp.concatenate([sums[d * 16 : d * 16 + 16, :] for d in range(digits)], axis=1)
    mid = dot3(rhs, f_hi[...], f_lo[...], NT)
    picked = dot3(mid, c_hi[...], c_lo[...], NN)

    def over(which):
        return lane_sum(jnp.where(which, total, 0.0))

    if final:
        own = lane == y_ref[0] * LANES + LOCAL
        energy = over(own) + lane_sum(mid * mid)
        wide = lax.broadcasted_iota(jnp.int32, picked.shape, 1)
        picked = jnp.where(wide == NORM, energy, picked)
        scal[...] = jnp.where(lane == 0, over(slot == CROSS), over(slot == SQUARE))
    else:
        scal[...] = jnp.broadcast_to(over(slot == NORM), (16, BW))
    part[...] = picked


def next_vector(
    slots, y_ref, z0, i0, i1, i2, i3, p0, p1, p2, p3, b_hi, b_lo, v0, bx_hi, bx_lo, weight, v1, pay
):
    picked = (p0[...] + p1[...]) + (p2[...] + p3[...])
    v1[...] = z0[...] + dot3(picked, b_hi[...], b_lo[...], NN)
    subtract_faces(v1, slots, (i0, i1, i2, i3))
    v = v1[...]
    w = v * weight[0:1, :]
    lane = lax.broadcasted_iota(jnp.int32, (16, BW), 1)
    y = y_ref[0]
    pay[...] = (
        dot3(v, bx_hi[...], bx_lo[...], NT)
        + place(lane, y, CROSS, lane_sum(v0[...] * w))
        + place(lane, y, SQUARE, lane_sum(v * w))
    )


def finish(slots, z1, i0, i1, i2, i3, p0, p1, p2, p3, b_hi, b_lo, v0, v1, s0, s1, mult, resid):
    picked = (p0[...] + p1[...]) + (p2[...] + p3[...])
    resid[...] = z1[...] + dot3(picked, b_hi[...], b_lo[...], NN)
    subtract_faces(resid, slots, (i0, i1, i2, i3))
    norm, cross, square = (s0[:, 0:1], s1[:, 0:1], s1[:, 1:2])
    energy = picked[:, NORM : NORM + 1]
    step1 = norm / cross
    fresh = norm - 2.0 * step1 * cross + step1 * step1 * square
    c = 1.0 + fresh / norm
    curvature = c * c * cross - 2.0 * c * step1 * square + step1 * step1 * energy
    step2 = fresh / curvature
    first, second = (v0[...], v1[...])
    mult[...] = (step1 + step2 * c) * first - (step2 * step1) * second
    resid[...] = first - (step1 + step2 * c) * second + (step2 * step1) * resid[...]


def call(kernel, name, ins, outs, scratch=(), mib=32, specs=None):
    return pl.pallas_call(
        kernel,
        out_shape=[jax.ShapeDtypeStruct(s, d) for s, d in outs],
        in_specs=specs,
        out_specs=[VMEM] * len(outs),
        scratch_shapes=[pltpu.VMEM(s, d) for s, d in scratch],
        compiler_params=params(mib),
        name=name,
    )(*ins)


def per_device(interface_load, flexibility, corner_coupling, coarse_factor, face_slots, corner_map):
    load = interface_load[0]
    matrix = flexibility[0]
    coupling = corner_coupling[0]
    slots = face_slots[0]
    cases, dofs = load.shape
    owned, coarse_dofs = coarse_factor.shape
    corners = coupling.shape[0]
    zs, xs = (lax.axis_size("z"), lax.axis_size("x"))
    subs = zs * xs * lax.axis_size("c")
    ys = lax.axis_size("y")
    face = 4 * BW
    y = lax.axis_index("y").astype(jnp.int32).reshape(1)

    def neighbours(o0, o1, o2, o3):
        back = [(i + 1, i) for i in range(subs - 1)]
        ahead = [(i, i + 1) for i in range(subs - 1)]
        left = [(j + 1, j) for j in range(ys - 1)]
        right = [(j, j + 1) for j in range(ys - 1)]
        return (
            lax.ppermute(o1, SUB, ahead),
            lax.ppermute(o0, SUB, back),
            lax.ppermute(o3, "y", right),
            lax.ppermute(o2, "y", left),
        )

    def others(p):
        return [lax.ppermute(p, "y", [(j, (j + k) % ys) for j in range(ys)]) for k in range(1, ys)]

    def gather_sub(p):
        every = jnp.broadcast_to(p[None], (zs * xs,) + p.shape)
        mine = lax.all_to_all(every, ("z", "x"), 0, 0)
        return mine, lax.ppermute(mine, "c", [(0, 1), (1, 0)])

    *faces, cm_row = call(
        first_pack,
        "first_pack",
        (slots, corner_map, y, load),
        [((24, face), F32)] * 2 + [((16, face), F32)] * 2 + [((8, BW), F32)],
        specs=[SMEM, SMEM, SMEM, VMEM],
    )
    got = neighbours(*faces)
    bx_hi, bx_lo, weight, f_hi, f_lo = call(
        prepare,
        "prepare",
        (slots, y, coupling, coarse_factor),
        [((BW, dofs), BF16)] * 2 + [((8, dofs), F32)] + [((owned, coarse_dofs), BF16)] * 2,
        [((BW, dofs), F32)],
        specs=[SMEM, SMEM, VMEM, VMEM],
    )
    v0, pay = call(
        first_vector,
        "first_vector",
        (slots, y, load, *got, bx_hi, bx_lo, weight, cm_row),
        [((cases, dofs), F32), ((24, BW), F32)],
        specs=[SMEM, SMEM] + [VMEM] * 9,
    )

    def product(first, v):
        width = 256
        rows = 40 if first else 16
        whole = pl.BlockSpec((cases, dofs), lambda j: (0, 0))
        outs = [((cases, dofs), F32)] + [((rows, face), F32)] * 4
        if not first:
            outs = outs + [((cases, BW), F32)]
        ins = (slots, y, v, matrix) + ((coupling,) if first else ())
        in_specs = [SMEM, SMEM, whole, pl.BlockSpec((dofs, width), lambda j: (0, j))]
        if first:
            in_specs = in_specs + [pl.BlockSpec((corners, dofs), lambda j: (0, 0))]
        return pl.pallas_call(
            functools.partial(local_product, first),
            grid=(dofs // width,),
            out_shape=[jax.ShapeDtypeStruct(s, d) for s, d in outs],
            in_specs=in_specs,
            out_specs=[pl.BlockSpec(s, lambda j: (0, 0)) for s, _ in outs],
            scratch_shapes=[pltpu.VMEM((2 * cases, dofs), BF16)],
            compiler_params=params(32),
            name="local_product",
        )(*ins)

    def solve(final, t, m):
        groups = 2 * t[0].shape[0]
        return call(
            functools.partial(coarse, final),
            "coarse",
            (y, *t, *m, f_hi, f_lo, c_hi, c_lo),
            [((cases, 3 * BW), F32), ((cases, BW), F32)],
            [
                ((2 * cases * (coarse_dofs // RADIX), groups * BW), BF16),
                ((RADIX, groups * BW), BF16),
            ],
            specs=[SMEM] + [VMEM] * 8,
        )

    row = sum(others(pay), pay)
    gathered = gather_sub(row)
    z0, *faces = product(True, v0)
    c_hi, c_lo = call(
        picked_columns,
        "picked_columns",
        (row, f_hi, f_lo),
        [((owned, 3 * BW), BF16)] * 2,
        specs=[VMEM] * 3,
    )
    got = neighbours(*faces)
    b_hi, b_lo = call(
        jumped_coupling,
        "jumped_coupling",
        (slots, y, coupling, *got),
        [((3 * BW, dofs), BF16)] * 2,
        [((3 * BW, dofs), F32)],
        specs=[SMEM, SMEM] + [VMEM] * 5,
    )
    part, scal0 = solve(False, gathered, gathered)
    v1, pay = call(
        next_vector,
        "next_vector",
        (slots, y, z0, *got, part, *others(part), b_hi, b_lo, v0, bx_hi, bx_lo, weight),
        [((cases, dofs), F32), ((cases, BW), F32)],
        specs=[SMEM, SMEM] + [VMEM] * 15,
    )
    z1, *faces, local_dot = product(False, v1)
    row = sum(others(pay), pay) + local_dot
    later = gather_sub(row)
    got = neighbours(*faces)
    part, scal1 = solve(True, later, gathered)
    mult, resid = call(
        finish,
        "finish",
        (slots, z1, *got, part, *others(part), b_hi, b_lo, v0, v1, scal0, scal1),
        [((cases, dofs), F32)] * 2,
        specs=[SMEM] + [VMEM] * 15,
    )
    return mult[None], resid[None]


def solution(mesh):
    fine = Mesh(mesh.devices.reshape(8, 4, 2, 4), ALL)
    in_specs = (
        P(ALL, None, None),
        P(ALL, None, None),
        P(ALL, None, None),
        P("y", None),
        P(ALL, None, None),
        P(ALL, None),
    )
    out_specs = (P(ALL, None, None), P(ALL, None, None))
    return jax.shard_map(
        per_device, mesh=fine, in_specs=in_specs, out_specs=out_specs, check_vma=False
    )
```

```python
import functools

import jax
import jax.numpy as jnp
from jax import lax
from jax.experimental import pallas as pl
from jax.experimental.pallas import tpu as pltpu
from jax.sharding import Mesh, PartitionSpec as P

BW = 128
LANES = 32
NORM, CROSS, SQUARE, LOCAL = 24, 25, 26, 27
MAP, PER = 26, 6
RADIX = 256
F32, BF16 = jnp.float32, jnp.bfloat16
ALL = ("z", "x", "c", "y")
SUB = ("z", "x", "c")
FETCH = 44

NN = (((1,), (0,)), ((), ()))
NT = (((1,), (1,)), ((), ()))

VMEM = pl.BlockSpec(memory_space=pltpu.VMEM)
SMEM = pl.BlockSpec(memory_space=pltpu.SMEM)


def split(x):
    hi = x.astype(BF16)
    return hi, (x - hi.astype(F32)).astype(BF16)


def dot(a, b, dims):
    return lax.dot_general(a, b, dims, preferred_element_type=F32)


def dot3(a, b_hi, b_lo, dims):
    rows = a.shape[0]
    a_hi, a_lo = split(a)
    both = dot(jnp.concatenate([a_hi, a_lo], axis=0), b_hi, dims)
    return both[:rows] + both[rows:] + dot(a_hi, b_lo, dims)


def block_at(b):
    return pl.ds(pl.multiple_of(jnp.maximum(b, 0) * BW, BW), BW)


def place_of(ints):
    return ints[ints.shape[0] - 2], ints[ints.shape[0] - 1]


def faces_of(ints):
    y, core = place_of(ints)
    odd = y % 2
    return (1 - core, core, 3 - odd, 2 + odd)


def subtract_faces(ref, ints, incoming):
    for f, (got, col0) in zip(faces_of(ints), incoming):
        for c in range(4):
            b = ints[f * 4 + c]
            at = block_at(b)
            held = ref[:, at]
            ref[:, at] = jnp.where(b >= 0, held - got[0:16, col0 + c * BW : col0 + (c + 1) * BW], held)


def pack_face(values, ints, f, out):
    rows = values.shape[0]
    for c in range(4):
        out[0:rows, c * BW : (c + 1) * BW] = values[:, block_at(ints[f * 4 + c])]


def lane_sum(x):
    return jnp.sum(x, axis=1, keepdims=True)


def place(lane, y, slot, column):
    return jnp.where(lane == y * LANES + slot, column, 0.0)


def first_pack(ints, both, o0, o1, o2, o3, own_map):
    row = lax.broadcasted_iota(jnp.int32, (8, BW), 0)
    lane = lax.broadcasted_iota(jnp.int32, (8, BW), 1) - (place_of(ints)[0] * LANES + MAP)
    placed = jnp.zeros((8, BW), jnp.int32)
    for j in range(24):
        here = jnp.logical_and(row == j // PER, lane == j % PER)
        placed = jnp.where(here, ints[16 + j], placed)
    placed = placed.astype(F32)
    own_map[...] = placed
    for f, o in zip(faces_of(ints), (o0, o1, o2, o3)):
        pack_face(both, ints, f, o)
    for o in (o0, o1):
        o[40:48, 0:BW] = placed
        o[40:48, BW:] = jnp.zeros((8, 3 * BW), F32)


def spread_coupling(ints, both, mat, bx_hi, bx_lo, weight, held, bx, sems):
    rows = mat.shape[0] // 4
    copies = []
    for n in range(4):
        at = pl.ds(n * rows, rows)
        copies.append(pltpu.make_async_copy(mat.at[at], held.at[at], sems.at[n]))
        copies[n].start()
    bx[...] = jnp.zeros_like(bx)
    bx[pl.ds(pl.multiple_of(place_of(ints)[0] * LANES, LANES), 24), :] = both[16:40, :]
    hi, lo = split(bx[...])
    bx_hi[...] = hi
    bx_lo[...] = lo
    weight[...] = jnp.ones_like(weight)
    for f in range(4):
        for c in range(4):
            b = ints[f * 4 + c]
            at = block_at(b)
            weight[:, at] = jnp.where(b >= 0, jnp.full((8, BW), 0.5, F32), weight[:, at])
    for copy in copies:
        copy.wait()


def first_vector(ints, both, i0, i1, i2, i3, bx_hi, bx_lo, weight, own_map, v0, pay):
    v0[...] = both[0:16, :]
    subtract_faces(v0, ints, [(i, 0) for i in (i0, i1, i2, i3)])
    v = v0[...]
    norm = lane_sum(v * v * weight[0:1, :])
    lane = lax.broadcasted_iota(jnp.int32, (16, BW), 1)
    maps = jnp.concatenate(
        [own_map[0:4, :], i0[40:44, 0:BW], i1[40:44, 0:BW], jnp.zeros((4, BW), F32)], axis=0
    )
    pay[...] = dot3(v, bx_hi[...], bx_lo[...], NT) + place(lane, place_of(ints)[0], NORM, norm) + maps


def local_product(final, ints, v, mat, z, o0, o1, o2, o3, *rest):
    width = 256
    hi, lo = split(v[...])
    pieces = jnp.concatenate([hi, lo], axis=0)
    for step in range(mat.shape[1] // width):
        at = slice(step * width, (step + 1) * width)
        both = dot(pieces, mat[:, at], NN)
        z[:, at] = both[:16] + both[16:]
    for f, o in zip(faces_of(ints), (o0, o1, o2, o3)):
        pack_face(z, ints, f, o)
    if final:
        (dot_out,) = rest
        lane = lax.broadcasted_iota(jnp.int32, (16, BW), 1)
        dot_out[...] = place(lane, place_of(ints)[0], LOCAL, lane_sum(v[...] * z[...]))


def jumped_coupling(ints, both, i0, i1, i2, i3, b_hi, b_lo, full):
    y = place_of(ints)[0]
    full[...] = jnp.zeros_like(full)

    def rows(n):
        return pl.ds(pl.multiple_of(n * LANES, LANES), 24)

    full[rows(y), :] = both[16:40, :]
    beside = y + 2 * (y % 2) - 1
    places = (rows(4), rows(5), rows(y + 1 - 2 * (y % 2)), rows(jnp.clip(beside, 0, 3)))
    for f, to, got in zip(faces_of(ints), places, (i0, i1, i2, i3)):
        for c in range(4):
            b = ints[f * 4 + c]
            at = block_at(b)
            full[to, at] = jnp.where(b >= 0, -got[16:40, c * BW : (c + 1) * BW], full[to, at])
    hi, lo = split(full[...])
    b_hi[...] = hi
    b_lo[...] = lo


def unpacked_map(rows):
    slot = lax.broadcasted_iota(jnp.int32, rows[0].shape, 1) % LANES
    found = jnp.zeros_like(rows[0])
    for k, row in enumerate(rows):
        found = jnp.where(slot // PER == k, pltpu.roll(row, BW - (MAP - PER * k), 1), found)
    return found.astype(jnp.int32), slot


def picked_columns(pay, f_hi, f_lo, c_hi, c_lo):
    dofs = f_hi.shape[1]
    wanted = []
    for n in range(3):
        rows = [jnp.broadcast_to(pay[4 * n + k : 4 * n + k + 1, :], (8, BW)) for k in range(4)]
        wanted.append(unpacked_map(rows)[0][0:1, :])
    wanted = jnp.concatenate(wanted, axis=1)
    row = lax.broadcasted_iota(jnp.int32, (dofs, 3 * BW), 0)
    hot = (row == wanted).astype(F32).astype(BF16)
    c_hi[...] = dot(f_hi[...], hot, NN).astype(BF16)
    c_lo[...] = dot(f_lo[...], hot, NN).astype(BF16)


def coarse_half(first, t, near, *rest):
    if first:
        factor, out, f_hi, f_lo, top, hot, terms_at = rest
    else:
        f_hi, f_lo, top, hot, out, terms_at = rest
    groups = t.shape[0]
    owned = f_hi.shape[0]
    digits = f_hi.shape[1] // RADIX
    half = digits * 16
    if first:
        dof, slot = unpacked_map([t[:, k, :] for k in range(4)])
        top[...] = jnp.where(slot < 24, dof // RADIX, -1).astype(F32)
        low = (dof % RADIX).astype(F32)
        low = jnp.transpose(jnp.concatenate([low] * (BW // groups), axis=0))
        lane = lax.broadcasted_iota(jnp.int32, (BW, BW), 1).astype(F32)
        one, zero = (jnp.ones((BW, BW), BF16), jnp.zeros((BW, BW), BF16))
        for j in range(groups):
            column = jnp.broadcast_to(low[:, j : j + 1], (BW, BW)).astype(BF16)
            for n in range(RADIX // BW):
                wanted = (lane + float(n * BW)).astype(BF16)
                hot[j * BW : (j + 1) * BW, n * BW : (n + 1) * BW] = jnp.where(
                    wanted == column, one, zero
                )
    none = jnp.zeros((16, BW), BF16)

    def body(j, acc):
        terms = t[j]
        digit = jnp.broadcast_to(top[pl.ds(j, 1), :], (16, BW)).astype(BF16)
        hi, lo = split(terms)
        at = pl.ds(pl.multiple_of(j * BW, BW), BW)
        for d in range(digits):
            mine = digit == jnp.full((16, BW), d, BF16)
            terms_at[d * 16 : d * 16 + 16, at] = jnp.where(mine, hi, none)
            terms_at[half + d * 16 : half + d * 16 + 16, at] = jnp.where(mine, lo, none)
        return acc + terms

    total = lax.fori_loop(0, groups, body, jnp.zeros((16, BW), F32), unroll=4)
    sums = dot(terms_at[...], hot[...], NN)
    sums = sums[:half] + sums[half:]
    rhs = jnp.concatenate([sums[d * 16 : d * 16 + 16, :] for d in range(digits)], axis=1)
    hi, lo = split(rhs)
    pieces = jnp.concatenate([hi, lo], axis=0)
    if first:
        f_hi[...], f_lo[...] = split(factor[...])
    column = lax.broadcasted_iota(jnp.int32, (owned, 32), 1)
    mid = dot(f_hi[...], pieces, NT) + jnp.where(column < 16, dot(f_lo[...], pieces, NT), 0.0)
    mid = jnp.transpose(mid)
    out[:, 0:owned] = mid[:16] + mid[16:]
    out[:, owned : owned + BW] = total
    out[:, owned + BW :] = near[...]


def coarse_part(final, ints, own, got, beside, c_hi, c_lo, out, scal):
    owned = c_hi.shape[0]
    mid = own[:, 0:owned] + got[:, 0:owned]
    total = own[:, owned : owned + BW] + got[:, owned : owned + BW]
    picked = dot3(mid, c_hi[...], c_lo[...], NN)
    lane = lax.broadcasted_iota(jnp.int32, (16, BW), 1)
    slot = lane % LANES

    def over(which):
        return lane_sum(jnp.where(which, total, 0.0))

    if final:
        energy = over(lane == place_of(ints)[0] * LANES + LOCAL) + lane_sum(mid * mid)
        wide = lax.broadcasted_iota(jnp.int32, picked.shape, 1)
        picked = jnp.where(wide == NORM, energy, picked)
        scal[...] = jnp.where(lane == 0, over(slot == CROSS), over(slot == SQUARE))
    else:
        scal[...] = jnp.broadcast_to(over(slot == NORM), (16, BW))
    width = picked.shape[1]
    out[:, 0:width] = picked
    out[:, width:] = beside[...]


def second_part(own, got, beside, out):
    width = own.shape[1] - beside.shape[1]
    out[:, 0:width] = own[:, 0:width] + got[:, 0:width]
    out[:, width:] = beside[...]


def jumped(out, z, ints, got, far, p1, sent, p2, b_hi, b_lo):
    width = sent.shape[1] - 4 * BW
    picked = sent[:, 0:width] + p2[:, 0:width]
    y = place_of(ints)[0]
    lane = lax.broadcasted_iota(jnp.int32, (16, BW), 1)
    beside = pltpu.roll(picked[:, BW : 2 * BW], (BW - y * LANES) % BW, 1)
    beyond = pltpu.roll(picked[:, 2 * BW :], (BW + LANES - y * LANES) % BW, 1)
    beside = jnp.where(lane < LANES, beside, jnp.where(lane < 2 * LANES, beyond, 0.0))
    needed = jnp.concatenate([picked[:, 0:BW], beside], axis=1)
    out[...] = z[...] + dot3(needed, b_hi[...], b_lo[...], NN)
    near_at = got.shape[1] - 4 * BW
    subtract_faces(out, ints, ((got, near_at), (far, 0), (p1, width), (p2, width)))
    return picked


def next_vector(
    ints, z0, got, far, p1, sent, p2, b_hi, b_lo, v0, bx_hi, bx_lo, weight, v1, pay
):
    jumped(v1, z0, ints, got, far, p1, sent, p2, b_hi, b_lo)
    v = v1[...]
    w = v * weight[0:1, :]
    lane = lax.broadcasted_iota(jnp.int32, (16, BW), 1)
    y = place_of(ints)[0]
    pay[...] = (
        dot3(v, bx_hi[...], bx_lo[...], NT)
        + place(lane, y, CROSS, lane_sum(v0[...] * w))
        + place(lane, y, SQUARE, lane_sum(v * w))
    )


def finish(ints, z1, got, far, p1, sent, p2, b_hi, b_lo, v0, v1, s0, s1, mult, resid):
    picked = jumped(resid, z1, ints, got, far, p1, sent, p2, b_hi, b_lo)
    norm, cross, square = (s0[:, 0:1], s1[:, 0:1], s1[:, 1:2])
    energy = picked[:, NORM : NORM + 1]
    step1 = norm / cross
    fresh = norm - 2.0 * step1 * cross + step1 * step1 * square
    c = 1.0 + fresh / norm
    curvature = c * c * cross - 2.0 * c * step1 * square + step1 * step1 * energy
    step2 = fresh / curvature
    first, second = (v0[...], v1[...])
    mult[...] = (step1 + step2 * c) * first - (step2 * step1) * second
    resid[...] = first - (step1 + step2 * c) * second + (step2 * step1) * resid[...]


def call(kernel, name, ins, outs, scalars, micros, scratch=(), mib=8, outside=()):
    specs = [SMEM] * scalars + [VMEM] * (len(ins) - scalars)
    for n in outside:
        specs[n] = pl.BlockSpec(memory_space=pl.ANY)
    return pl.pallas_call(
        kernel,
        out_shape=[jax.ShapeDtypeStruct(s, d) for s, d in outs],
        in_specs=specs,
        out_specs=[VMEM] * len(outs),
        scratch_shapes=[pltpu.VMEM(*s) if isinstance(s, tuple) else s for s in scratch],
        compiler_params=pltpu.CompilerParams(vmem_limit_bytes=mib * 1024 * 1024),
        cost_estimate=pl.CostEstimate(
            flops=int(micros * 1e6), bytes_accessed=int(micros * 3.5e6), transcendentals=0
        ),
        name=name,
    )(*ins)


def per_device(interface_load, flexibility, corner_coupling, coarse_factor, face_slots, corner_map):
    both = jnp.concatenate([interface_load[0], corner_coupling[0]], axis=0)
    cases, dofs = interface_load.shape[1:]
    owned, coarse_dofs = coarse_factor.shape
    zs, xs, cs, ys = (lax.axis_size(a) for a in ALL)
    subs = zs * xs * cs
    face = 4 * BW
    here = jnp.stack([lax.axis_index("y"), lax.axis_index("c")]).astype(jnp.int32)
    ints = jnp.concatenate([*(face_slots[0, f] for f in range(4)), corner_map[0], here])
    near_pairs = [(i, i ^ 1) for i in range(cs)]
    far_pairs = [(i, (i + 1) % subs) for i in range(1, subs, 2)]
    far_pairs = far_pairs + [(j, i) for i, j in far_pairs]
    one_pairs = [(j, j ^ 1) for j in range(ys)]
    two_pairs = [(j, j ^ 3) for j in range(ys)]

    def near(p):
        return lax.ppermute(p, "c", near_pairs)

    def far(p):
        return lax.ppermute(p, SUB, far_pairs)

    def one(p):
        return lax.ppermute(p, "y", one_pairs)

    def two(p):
        return lax.ppermute(p, "y", two_pairs)

    def gather(row):
        every = jnp.broadcast_to(row[None], (zs * xs,) + row.shape)
        return lax.all_to_all(every, ("z", "x"), 0, 0)

    def product(final, v):
        outs = [((cases, dofs), F32)] + [((cases, face), F32)] * 4
        if final:
            outs = outs + [((cases, BW), F32)]
        return call(
            functools.partial(local_product, final),
            "local_product",
            (ints, v, matrix),
            outs,
            1,
            2,
            mib=6,
        )

    def half(first, t, face_near, *held):
        terms = t.shape[0] * BW
        outs = [((cases, owned + BW + face), F32)]
        if first:
            outs = outs + [((owned, coarse_dofs), BF16)] * 2
            outs = outs + [((t.shape[0], BW), F32), ((terms, RADIX), BF16)]
        return call(
            functools.partial(coarse_half, first),
            "coarse_half",
            (t, face_near, *held),
            outs,
            0,
            4,
            [((2 * cases * (coarse_dofs // RADIX), terms), BF16)],
            mib=16,
        )

    def rest_of_solve(final, own, face_one, face_two, *early):
        got = near(own)
        sent, scal = call(
            functools.partial(coarse_part, final),
            "coarse_part",
            (ints, own, got, face_one, c_hi, c_lo),
            [((cases, 3 * BW + face), F32), ((cases, BW), F32)],
            1,
            1,
        )
        p1, *early = lax.optimization_barrier((one(sent), *early))
        (sent,) = call(
            second_part, "second_part", (sent, p1, face_two), [((cases, 3 * BW + face), F32)], 0, 0.5
        )
        return early, scal, got, p1, sent, two(sent)

    o0, o1, o2, o3, own_map = call(
        first_pack,
        "first_pack",
        (ints, both),
        [((48, face), F32)] * 2 + [((40, face), F32)] * 2 + [((8, BW), F32)],
        1,
        1,
    )
    far_came = far(o1)
    came = (near(o0), far_came, one(o2), two(o3))
    bx_hi, bx_lo, weight, matrix = call(
        spread_coupling,
        "spread_coupling",
        (ints, both, flexibility[0]),
        [((BW, dofs), BF16)] * 2 + [((8, dofs), F32), ((dofs, dofs), BF16)],
        1,
        3,
        [((BW, dofs), F32), pltpu.SemaphoreType.DMA((4,))],
        mib=FETCH,
        outside=(2,),
    )
    v0, pay = call(
        first_vector,
        "first_vector",
        (ints, both, *came, bx_hi, bx_lo, weight, own_map),
        [((cases, dofs), F32), ((cases, BW), F32)],
        1,
        1,
    )
    came_one, z0, *faces = lax.optimization_barrier((one(pay), *product(False, v0)))
    pair = pay + came_one
    row = pair + two(pair)
    terms0, face_far = lax.optimization_barrier((gather(row), faces[1]))
    face_far = far(face_far)
    own, *held = half(True, terms0, faces[0], coarse_factor)
    f_hi, f_lo = held[:2]
    c_hi, c_lo = call(
        picked_columns,
        "picked_columns",
        (row, f_hi, f_lo),
        [((owned, 3 * BW), BF16)] * 2,
        0,
        2.5,
        mib=16,
    )
    b_hi, b_lo = call(
        jumped_coupling,
        "jumped_coupling",
        (ints, both, *came),
        [((2 * BW, dofs), BF16)] * 2,
        1,
        1.2,
        [((2 * BW, dofs), F32)],
        mib=10,
    )
    (b_hi, b_lo), scal0, got, *parts = rest_of_solve(False, own, faces[2], faces[3], b_hi, b_lo)
    v1, pay = call(
        next_vector,
        "next_vector",
        (ints, z0, got, face_far, *parts, b_hi, b_lo, v0, bx_hi, bx_lo, weight),
        [((cases, dofs), F32), ((cases, BW), F32)],
        1,
        1.6,
        mib=12,
    )
    came_one, z1, *faces, local_dot = lax.optimization_barrier((one(pay), *product(True, v1)))
    pair = pay + came_one
    row = pair + two(pair) + local_dot
    terms1, face_far = lax.optimization_barrier((gather(row), faces[1]))
    face_far = far(face_far)
    (own,) = half(False, terms1, faces[0], *held)
    _, scal1, got, *parts = rest_of_solve(True, own, faces[2], faces[3])
    mult, resid = call(
        finish,
        "finish",
        (ints, z1, got, face_far, *parts, b_hi, b_lo, v0, v1, scal0, scal1),
        [((cases, dofs), F32)] * 2,
        1,
        1.9,
        mib=12,
    )
    return mult[None], resid[None]


def solution(mesh):
    fine = Mesh(mesh.devices.reshape(8, 4, 2, 4), ALL)
    in_specs = (
        P(ALL, None, None),
        P(ALL, None, None),
        P(ALL, None, None),
        P("y", None),
        P(ALL, None, None),
        P(ALL, None),
    )
    out_specs = (P(ALL, None, None), P(ALL, None, None))
    return jax.shard_map(
        per_device, mesh=fine, in_specs=in_specs, out_specs=out_specs, check_vma=False
    )
```

```python
import functools

import jax
import jax.numpy as jnp
from jax import lax
from jax.experimental import pallas as pl
from jax.experimental.pallas import tpu as pltpu
from jax.sharding import Mesh, PartitionSpec as P

BW = 128
LANES = 32
NORM, CROSS, SQUARE, LOCAL = 24, 25, 26, 27
MAP, PER = 26, 6
RADIX = 256
F32, BF16 = jnp.float32, jnp.bfloat16
ALL = ("z", "x", "c", "y")
SUB = ("z", "x", "c")
FETCH = 44
CHUNKS = 16

NN = (((1,), (0,)), ((), ()))
NT = (((1,), (1,)), ((), ()))

VMEM = pl.BlockSpec(memory_space=pltpu.VMEM)
SMEM = pl.BlockSpec(memory_space=pltpu.SMEM)


def split(x):
    hi = x.astype(BF16)
    return hi, (x - hi.astype(F32)).astype(BF16)


def dot(a, b, dims):
    return lax.dot_general(a, b, dims, preferred_element_type=F32)


def dot3(a, b_hi, b_lo, dims):
    rows = a.shape[0]
    a_hi, a_lo = split(a)
    both = dot(jnp.concatenate([a_hi, a_lo], axis=0), b_hi, dims)
    return both[:rows] + both[rows:] + dot(a_hi, b_lo, dims)


def block_at(b):
    return pl.ds(pl.multiple_of(jnp.maximum(b, 0) * BW, BW), BW)


def place_of(ints):
    return ints[ints.shape[0] - 2], ints[ints.shape[0] - 1]


def faces_of(ints):
    y, core = place_of(ints)
    odd = y % 2
    return (1 - core, core, 3 - odd, 2 + odd)


def subtract_faces(ref, ints, incoming):
    for f, (got, col0) in zip(faces_of(ints), incoming):
        for c in range(4):
            b = ints[f * 4 + c]
            at = block_at(b)
            held = ref[:, at]
            ref[:, at] = jnp.where(b >= 0, held - got[0:16, col0 + c * BW : col0 + (c + 1) * BW], held)


def pack_face(values, ints, f, out):
    rows = values.shape[0]
    for c in range(4):
        out[0:rows, c * BW : (c + 1) * BW] = values[:, block_at(ints[f * 4 + c])]


def lane_sum(x):
    return jnp.sum(x, axis=1, keepdims=True)


def place(lane, y, slot, column):
    return jnp.where(lane == y * LANES + slot, column, 0.0)


def first_pack(ints, both, o0, o1, o2, o3, own_map):
    row = lax.broadcasted_iota(jnp.int32, (8, BW), 0)
    lane = lax.broadcasted_iota(jnp.int32, (8, BW), 1) - (place_of(ints)[0] * LANES + MAP)
    placed = jnp.zeros((8, BW), jnp.int32)
    for j in range(24):
        here = jnp.logical_and(row == j // PER, lane == j % PER)
        placed = jnp.where(here, ints[16 + j], placed)
    placed = placed.astype(F32)
    own_map[...] = placed
    for f, o in zip(faces_of(ints), (o0, o1, o2, o3)):
        pack_face(both, ints, f, o)
    for o in (o0, o1):
        o[40:48, 0:BW] = placed
        o[40:48, BW:] = jnp.zeros((8, 3 * BW), F32)


def spread_coupling(ints, both, mat, bx_hi, bx_lo, weight, held, bx, sems):
    rows = mat.shape[0] // CHUNKS
    copies = []
    for n in range(CHUNKS):
        at = pl.ds(n * rows, rows)
        copies.append(pltpu.make_async_copy(mat.at[at], held.at[at], sems.at[n]))
        copies[n].start()
    bx[...] = jnp.zeros_like(bx)
    bx[pl.ds(pl.multiple_of(place_of(ints)[0] * LANES, LANES), 24), :] = both[16:40, :]
    hi, lo = split(bx[...])
    bx_hi[...] = hi
    bx_lo[...] = lo
    weight[...] = jnp.ones_like(weight)
    for f in range(4):
        for c in range(4):
            b = ints[f * 4 + c]
            at = block_at(b)
            weight[:, at] = jnp.where(b >= 0, jnp.full((8, BW), 0.5, F32), weight[:, at])
    for copy in copies:
        copy.wait()


def first_vector(ints, both, i0, i1, i2, i3, bx_hi, bx_lo, weight, own_map, v0, pay):
    v0[...] = both[0:16, :]
    subtract_faces(v0, ints, [(i, 0) for i in (i0, i1, i2, i3)])
    v = v0[...]
    norm = lane_sum(v * v * weight[0:1, :])
    lane = lax.broadcasted_iota(jnp.int32, (16, BW), 1)
    maps = jnp.concatenate(
        [own_map[0:4, :], i0[40:44, 0:BW], i1[40:44, 0:BW], jnp.zeros((4, BW), F32)], axis=0
    )
    pay[...] = dot3(v, bx_hi[...], bx_lo[...], NT) + place(lane, place_of(ints)[0], NORM, norm) + maps


def local_product(final, ints, v, mat, z, o0, o1, o2, o3, *rest):
    width = 256
    hi, lo = split(v[...])
    pieces = jnp.concatenate([hi, lo], axis=0)
    for step in range(mat.shape[1] // width):
        at = slice(step * width, (step + 1) * width)
        both = dot(pieces, mat[:, at], NN)
        z[:, at] = both[:16] + both[16:]
    for f, o in zip(faces_of(ints), (o0, o1, o2, o3)):
        pack_face(z, ints, f, o)
    if final:
        (dot_out,) = rest
        lane = lax.broadcasted_iota(jnp.int32, (16, BW), 1)
        dot_out[...] = place(lane, place_of(ints)[0], LOCAL, lane_sum(v[...] * z[...]))


def jumped_coupling(ints, both, i0, i1, i2, i3, b_hi, b_lo, full):
    y = place_of(ints)[0]
    full[...] = jnp.zeros_like(full)

    def rows(n):
        return pl.ds(pl.multiple_of(n * LANES, LANES), 24)

    full[rows(y), :] = both[16:40, :]
    beside = y + 2 * (y % 2) - 1
    places = (rows(4), rows(5), rows(y + 1 - 2 * (y % 2)), rows(jnp.clip(beside, 0, 3)))
    for f, to, got in zip(faces_of(ints), places, (i0, i1, i2, i3)):
        for c in range(4):
            b = ints[f * 4 + c]
            at = block_at(b)
            full[to, at] = jnp.where(b >= 0, -got[16:40, c * BW : (c + 1) * BW], full[to, at])
    hi, lo = split(full[...])
    b_hi[...] = hi
    b_lo[...] = lo


def unpacked_map(rows):
    slot = lax.broadcasted_iota(jnp.int32, rows[0].shape, 1) % LANES
    found = jnp.zeros_like(rows[0])
    for k, row in enumerate(rows):
        found = jnp.where(slot // PER == k, pltpu.roll(row, BW - (MAP - PER * k), 1), found)
    return found.astype(jnp.int32), slot


def picked_columns(pay, f_hi, f_lo, c_hi, c_lo):
    dofs = f_hi.shape[1]
    wanted = []
    for n in range(3):
        rows = [jnp.broadcast_to(pay[4 * n + k : 4 * n + k + 1, :], (8, BW)) for k in range(4)]
        wanted.append(unpacked_map(rows)[0][0:1, :])
    wanted = jnp.concatenate(wanted, axis=1)
    row = lax.broadcasted_iota(jnp.int32, (dofs, 3 * BW), 0)
    hot = (row == wanted).astype(F32).astype(BF16)
    c_hi[...] = dot(f_hi[...], hot, NN).astype(BF16)
    c_lo[...] = dot(f_lo[...], hot, NN).astype(BF16)


def coarse_half(first, t, near, *rest):
    if first:
        factor, out, f_hi, f_lo, top, hot, terms_at = rest
    else:
        f_hi, f_lo, top, hot, out, terms_at = rest
    groups = t.shape[0]
    owned = f_hi.shape[0]
    digits = f_hi.shape[1] // RADIX
    half = digits * 16
    if first:
        dof, slot = unpacked_map([t[:, k, :] for k in range(4)])
        top[...] = jnp.where(slot < 24, dof // RADIX, -1).astype(F32)
        low = (dof % RADIX).astype(F32)
        low = jnp.transpose(jnp.concatenate([low] * (BW // groups), axis=0))
        lane = lax.broadcasted_iota(jnp.int32, (BW, BW), 1).astype(F32)
        one, zero = (jnp.ones((BW, BW), BF16), jnp.zeros((BW, BW), BF16))
        for j in range(groups):
            column = jnp.broadcast_to(low[:, j : j + 1], (BW, BW)).astype(BF16)
            for n in range(RADIX // BW):
                wanted = (lane + float(n * BW)).astype(BF16)
                hot[j * BW : (j + 1) * BW, n * BW : (n + 1) * BW] = jnp.where(
                    wanted == column, one, zero
                )
    none = jnp.zeros((16, BW), BF16)

    def body(j, acc):
        terms = t[j]
        digit = jnp.broadcast_to(top[pl.ds(j, 1), :], (16, BW)).astype(BF16)
        hi, lo = split(terms)
        at = pl.ds(pl.multiple_of(j * BW, BW), BW)
        for d in range(digits):
            mine = digit == jnp.full((16, BW), d, BF16)
            terms_at[d * 16 : d * 16 + 16, at] = jnp.where(mine, hi, none)
            terms_at[half + d * 16 : half + d * 16 + 16, at] = jnp.where(mine, lo, none)
        return acc + terms

    total = lax.fori_loop(0, groups, body, jnp.zeros((16, BW), F32), unroll=4)
    sums = dot(terms_at[...], hot[...], NN)
    sums = sums[:half] + sums[half:]
    rhs = jnp.concatenate([sums[d * 16 : d * 16 + 16, :] for d in range(digits)], axis=1)
    hi, lo = split(rhs)
    pieces = jnp.concatenate([hi, lo], axis=0)
    if first:
        f_hi[...], f_lo[...] = split(factor[...])
    column = lax.broadcasted_iota(jnp.int32, (owned, 32), 1)
    mid = dot(f_hi[...], pieces, NT) + jnp.where(column < 16, dot(f_lo[...], pieces, NT), 0.0)
    mid = jnp.transpose(mid)
    out[:, 0:owned] = mid[:16] + mid[16:]
    out[:, owned : owned + BW] = total
    out[:, owned + BW :] = near[...]


def coarse_part(final, ints, own, got, face_one, face_two, c_hi, c_lo, part, out_one, out_two, scal):
    owned = c_hi.shape[0]
    mid = own[:, 0:owned] + got[:, 0:owned]
    total = own[:, owned : owned + BW] + got[:, owned : owned + BW]
    picked = dot3(mid, c_hi[...], c_lo[...], NN)
    lane = lax.broadcasted_iota(jnp.int32, (16, BW), 1)
    slot = lane % LANES

    def over(which):
        return lane_sum(jnp.where(which, total, 0.0))

    if final:
        energy = over(lane == place_of(ints)[0] * LANES + LOCAL) + lane_sum(mid * mid)
        wide = lax.broadcasted_iota(jnp.int32, picked.shape, 1)
        picked = jnp.where(wide == NORM, energy, picked)
        scal[...] = jnp.where(lane == 0, over(slot == CROSS), over(slot == SQUARE))
    else:
        scal[...] = jnp.broadcast_to(over(slot == NORM), (16, BW))
    width = picked.shape[1]
    part[...] = picked
    for out, beside in ((out_one, face_one), (out_two, face_two)):
        out[:, 0:width] = picked
        out[:, width:] = beside[...]


def jumped(out, z, ints, got, far, p0, p1, p2, p3, b_hi, b_lo):
    width = p0.shape[1]
    picked = (p0[...] + p1[:, 0:width]) + (p2[...] + p3[:, 0:width])
    y = place_of(ints)[0]
    lane = lax.broadcasted_iota(jnp.int32, (16, BW), 1)
    beside = pltpu.roll(picked[:, BW : 2 * BW], (BW - y * LANES) % BW, 1)
    beyond = pltpu.roll(picked[:, 2 * BW :], (BW + LANES - y * LANES) % BW, 1)
    beside = jnp.where(lane < LANES, beside, jnp.where(lane < 2 * LANES, beyond, 0.0))
    needed = jnp.concatenate([picked[:, 0:BW], beside], axis=1)
    out[...] = z[...] + dot3(needed, b_hi[...], b_lo[...], NN)
    near_at = got.shape[1] - 4 * BW
    subtract_faces(out, ints, ((got, near_at), (far, 0), (p1, width), (p3, width)))
    return picked


def next_vector(
    ints, z0, got, far, p0, p1, p2, p3, b_hi, b_lo, v0, bx_hi, bx_lo, weight, v1, pay
):
    jumped(v1, z0, ints, got, far, p0, p1, p2, p3, b_hi, b_lo)
    v = v1[...]
    w = v * weight[0:1, :]
    lane = lax.broadcasted_iota(jnp.int32, (16, BW), 1)
    y = place_of(ints)[0]
    pay[...] = (
        dot3(v, bx_hi[...], bx_lo[...], NT)
        + place(lane, y, CROSS, lane_sum(v0[...] * w))
        + place(lane, y, SQUARE, lane_sum(v * w))
    )


def finish(ints, z1, got, far, p0, p1, p2, p3, b_hi, b_lo, v0, v1, s0, s1, mult, resid):
    picked = jumped(resid, z1, ints, got, far, p0, p1, p2, p3, b_hi, b_lo)
    norm, cross, square = (s0[:, 0:1], s1[:, 0:1], s1[:, 1:2])
    energy = picked[:, NORM : NORM + 1]
    step1 = norm / cross
    fresh = norm - 2.0 * step1 * cross + step1 * step1 * square
    c = 1.0 + fresh / norm
    curvature = c * c * cross - 2.0 * c * step1 * square + step1 * step1 * energy
    step2 = fresh / curvature
    first, second = (v0[...], v1[...])
    mult[...] = (step1 + step2 * c) * first - (step2 * step1) * second
    resid[...] = first - (step1 + step2 * c) * second + (step2 * step1) * resid[...]


def call(kernel, name, ins, outs, scalars, micros, scratch=(), mib=8, outside=()):
    specs = [SMEM] * scalars + [VMEM] * (len(ins) - scalars)
    for n in outside:
        specs[n] = pl.BlockSpec(memory_space=pl.ANY)
    return pl.pallas_call(
        kernel,
        out_shape=[jax.ShapeDtypeStruct(s, d) for s, d in outs],
        in_specs=specs,
        out_specs=[VMEM] * len(outs),
        scratch_shapes=[pltpu.VMEM(*s) if isinstance(s, tuple) else s for s in scratch],
        compiler_params=pltpu.CompilerParams(vmem_limit_bytes=mib * 1024 * 1024),
        cost_estimate=pl.CostEstimate(
            flops=int(micros * 1e6), bytes_accessed=int(micros * 3.5e6), transcendentals=0
        ),
        name=name,
    )(*ins)


def per_device(interface_load, flexibility, corner_coupling, coarse_factor, face_slots, corner_map):
    both = jnp.concatenate([interface_load[0], corner_coupling[0]], axis=0)
    cases, dofs = interface_load.shape[1:]
    owned, coarse_dofs = coarse_factor.shape
    zs, xs, cs, ys = (lax.axis_size(a) for a in ALL)
    subs = zs * xs * cs
    face = 4 * BW
    here = jnp.stack([lax.axis_index("y"), lax.axis_index("c")]).astype(jnp.int32)
    ints = jnp.concatenate([*(face_slots[0, f] for f in range(4)), corner_map[0], here])
    near_pairs = [(i, i ^ 1) for i in range(cs)]
    far_pairs = [(i, (i + 1) % subs) for i in range(1, subs, 2)]
    far_pairs = far_pairs + [(j, i) for i, j in far_pairs]
    one_pairs = [(j, j ^ 1) for j in range(ys)]
    across_pairs = [(j, j ^ 2) for j in range(ys)]
    two_pairs = [(j, j ^ 3) for j in range(ys)]

    def near(p):
        return lax.ppermute(p, "c", near_pairs)

    def far(p):
        return lax.ppermute(p, SUB, far_pairs)

    def one(p):
        return lax.ppermute(p, "y", one_pairs)

    def across(p):
        return lax.ppermute(p, "y", across_pairs)

    def two(p):
        return lax.ppermute(p, "y", two_pairs)

    def gather(row):
        every = jnp.broadcast_to(row[None], (zs * xs,) + row.shape)
        return lax.all_to_all(every, ("z", "x"), 0, 0)

    def product(final, v):
        outs = [((cases, dofs), F32)] + [((cases, face), F32)] * 4
        if final:
            outs = outs + [((cases, BW), F32)]
        return call(
            functools.partial(local_product, final),
            "local_product",
            (ints, v, matrix),
            outs,
            1,
            2,
            mib=6,
        )

    def half(first, t, face_near, *held):
        terms = t.shape[0] * BW
        outs = [((cases, owned + BW + face), F32)]
        if first:
            outs = outs + [((owned, coarse_dofs), BF16)] * 2
            outs = outs + [((t.shape[0], BW), F32), ((terms, RADIX), BF16)]
        return call(
            functools.partial(coarse_half, first),
            "coarse_half",
            (t, face_near, *held),
            outs,
            0,
            4,
            [((2 * cases * (coarse_dofs // RADIX), terms), BF16)],
            mib=16,
        )

    def rest_of_solve(final, own, face_one, face_two):
        got = near(own)
        wide = 3 * BW
        part, out_one, out_two, scal = call(
            functools.partial(coarse_part, final),
            "coarse_part",
            (ints, own, got, face_one, face_two, c_hi, c_lo),
            [((cases, wide), F32)] + [((cases, wide + face), F32)] * 2 + [((cases, BW), F32)],
            1,
            1,
        )
        return scal, got, part, one(out_one), across(part), two(out_two)

    o0, o1, o2, o3, own_map = call(
        first_pack,
        "first_pack",
        (ints, both),
        [((48, face), F32)] * 2 + [((40, face), F32)] * 2 + [((8, BW), F32)],
        1,
        1,
    )
    far_came = far(o1)
    came = (near(o0), far_came, one(o2), two(o3))
    bx_hi, bx_lo, weight, matrix = call(
        spread_coupling,
        "spread_coupling",
        (ints, both, flexibility[0]),
        [((BW, dofs), BF16)] * 2 + [((8, dofs), F32), ((dofs, dofs), BF16)],
        1,
        3,
        [((BW, dofs), F32), pltpu.SemaphoreType.DMA((CHUNKS,))],
        mib=FETCH,
        outside=(2,),
    )
    v0, pay = call(
        first_vector,
        "first_vector",
        (ints, both, *came, bx_hi, bx_lo, weight, own_map),
        [((cases, dofs), F32), ((cases, BW), F32)],
        1,
        1,
    )
    rows = (across(pay), one(pay), two(pay))
    *rows, z0, n0, f0, a0, b0 = lax.optimization_barrier((*rows, *product(False, v0)))
    faces = (n0, f0, a0, b0)
    row = (pay + rows[0]) + (rows[1] + rows[2])
    terms0, face_far = lax.optimization_barrier((gather(row), faces[1]))
    face_far = far(face_far)
    own, *held = half(True, terms0, faces[0], coarse_factor)
    f_hi, f_lo = held[:2]
    c_hi, c_lo = call(
        picked_columns,
        "picked_columns",
        (row, f_hi, f_lo),
        [((owned, 3 * BW), BF16)] * 2,
        0,
        2.5,
        mib=16,
    )
    b_hi, b_lo = call(
        jumped_coupling,
        "jumped_coupling",
        (ints, both, *came),
        [((2 * BW, dofs), BF16)] * 2,
        1,
        1.2,
        [((2 * BW, dofs), F32)],
        mib=10,
    )
    scal0, got, *parts = rest_of_solve(False, own, faces[2], faces[3])
    v1, pay = call(
        next_vector,
        "next_vector",
        (ints, z0, got, face_far, *parts, b_hi, b_lo, v0, bx_hi, bx_lo, weight),
        [((cases, dofs), F32), ((cases, BW), F32)],
        1,
        1.6,
        mib=12,
    )
    rows = (across(pay), one(pay), two(pay))
    *rows, z1, n1, f1, a1, b1, local_dot = lax.optimization_barrier((*rows, *product(True, v1)))
    faces = (n1, f1, a1, b1)
    row = (pay + rows[0]) + (rows[1] + rows[2]) + local_dot
    terms1, face_far = lax.optimization_barrier((gather(row), faces[1]))
    face_far = far(face_far)
    (own,) = half(False, terms1, faces[0], *held)
    scal1, got, *parts = rest_of_solve(True, own, faces[2], faces[3])
    mult, resid = call(
        finish,
        "finish",
        (ints, z1, got, face_far, *parts, b_hi, b_lo, v0, v1, scal0, scal1),
        [((cases, dofs), F32)] * 2,
        1,
        1.9,
        mib=12,
    )
    return mult[None], resid[None]


def solution(mesh):
    fine = Mesh(mesh.devices.reshape(8, 4, 2, 4), ALL)
    in_specs = (
        P(ALL, None, None),
        P(ALL, None, None),
        P(ALL, None, None),
        P("y", None),
        P(ALL, None, None),
        P(ALL, None),
    )
    out_specs = (P(ALL, None, None), P(ALL, None, None))
    return jax.shard_map(
        per_device, mesh=fine, in_specs=in_specs, out_specs=out_specs, check_vma=False
    )
```

```python
import functools

import jax
import jax.numpy as jnp
from jax import lax
from jax.experimental import pallas as pl
from jax.experimental.pallas import tpu as pltpu
from jax.sharding import Mesh, PartitionSpec as P

BW = 128
LANES = 32
NORM, CROSS, SQUARE, LOCAL = 24, 25, 26, 27
MAP, PER = 26, 6
RADIX = 256
F32, BF16 = jnp.float32, jnp.bfloat16
ALL = ("z", "x", "c", "y")
SUB = ("z", "x", "c")
FETCH = 44
CHUNKS = 8

NN = (((1,), (0,)), ((), ()))
NT = (((1,), (1,)), ((), ()))

VMEM = pl.BlockSpec(memory_space=pltpu.VMEM)
SMEM = pl.BlockSpec(memory_space=pltpu.SMEM)


def split(x):
    hi = x.astype(BF16)
    return hi, (x - hi.astype(F32)).astype(BF16)


def dot(a, b, dims):
    return lax.dot_general(a, b, dims, preferred_element_type=F32)


def dot3(a, b_hi, b_lo, dims):
    rows = a.shape[0]
    a_hi, a_lo = split(a)
    both = dot(jnp.concatenate([a_hi, a_lo], axis=0), b_hi, dims)
    return both[:rows] + both[rows:] + dot(a_hi, b_lo, dims)


def block_at(b):
    return pl.ds(pl.multiple_of(jnp.maximum(b, 0) * BW, BW), BW)


def place_of(ints):
    return ints[0, 40], ints[0, 41]


def faces_of(ints):
    y, core = place_of(ints)
    odd = y % 2
    return (1 - core, core, 3 - odd, 2 + odd)


def subtract_faces(ref, ints, incoming):
    for f, (got, col0) in zip(faces_of(ints), incoming):
        for c in range(4):
            b = ints[0, f * 4 + c]
            at = block_at(b)
            held = ref[:, at]
            ref[:, at] = jnp.where(b >= 0, held - got[0:16, col0 + c * BW : col0 + (c + 1) * BW], held)


def pack_face(values, ints, f, out):
    rows = values.shape[0]
    for c in range(4):
        out[0:rows, c * BW : (c + 1) * BW] = values[:, block_at(ints[0, f * 4 + c])]


def lane_sum(x):
    return jnp.sum(x, axis=1, keepdims=True)


def place(lane, y, slot, column):
    return jnp.where(lane == y * LANES + slot, column, 0.0)


def first_pack(table, both, o0, o1, o2, o3, own_map, ints):
    flat = [table[f, c] for f in range(4) for c in range(4)]
    flat = flat + [table[4, j] for j in range(24)] + [table[5, 0], table[5, 1]]
    row = lax.broadcasted_iota(jnp.int32, (8, BW), 0)
    at = lax.broadcasted_iota(jnp.int32, (8, BW), 1)
    every = jnp.zeros((8, BW), jnp.int32)
    for n, value in enumerate(flat):
        every = jnp.where(at == n, value, every)
    ints[...] = every[0:1, :]
    y, core = (flat[40], flat[41])
    lane = at - (y * LANES + MAP)
    placed = jnp.zeros((8, BW), jnp.int32)
    for j in range(24):
        here = jnp.logical_and(row == j // PER, lane == j % PER)
        placed = jnp.where(here, flat[16 + j], placed)
    placed = placed.astype(F32)
    own_map[...] = placed
    for f, o in zip((1 - core, core, 3 - y % 2, 2 + y % 2), (o0, o1, o2, o3)):
        for c in range(4):
            o[0:40, c * BW : (c + 1) * BW] = both[:, block_at(table[f, c])]
    for o in (o0, o1):
        o[40:48, 0:BW] = placed
        o[40:48, BW:] = jnp.zeros((8, 3 * BW), F32)


def fetches(mat, row0, held, sems):
    rows = held.shape[0] // CHUNKS
    copies = []
    for n in range(CHUNKS):
        copies.append(
            pltpu.make_async_copy(
                mat.at[pl.ds(row0 + n * rows, rows)], held.at[pl.ds(n * rows, rows)], sems.at[n]
            )
        )
        copies[n].start()
    return copies


def spread_coupling(ints, both, mat, bx_hi, bx_lo, weight, held, bx, sems):
    copies = fetches(mat, 0, held, sems)
    bx[...] = jnp.zeros_like(bx)
    bx[pl.ds(pl.multiple_of(place_of(ints)[0] * LANES, LANES), 24), :] = both[16:40, :]
    hi, lo = split(bx[...])
    bx_hi[...] = hi
    bx_lo[...] = lo
    weight[...] = jnp.ones_like(weight)
    for f in range(4):
        for c in range(4):
            b = ints[0, f * 4 + c]
            at = block_at(b)
            weight[:, at] = jnp.where(b >= 0, jnp.full((8, BW), 0.5, F32), weight[:, at])
    for copy in copies:
        copy.wait()


def first_vector(ints, both, i0, i1, i2, i3, bx_hi, bx_lo, weight, own_map, v0, pay):
    v0[...] = both[0:16, :]
    subtract_faces(v0, ints, [(i, 0) for i in (i0, i1, i2, i3)])
    v = v0[...]
    norm = lane_sum(v * v * weight[0:1, :])
    lane = lax.broadcasted_iota(jnp.int32, (16, BW), 1)
    maps = jnp.concatenate(
        [own_map[0:4, :], i0[40:44, 0:BW], i1[40:44, 0:BW], jnp.zeros((4, BW), F32)], axis=0
    )
    pay[...] = dot3(v, bx_hi[...], bx_lo[...], NT) + place(lane, place_of(ints)[0], NORM, norm) + maps


def local_product(final, ints, v, top, bottom, z, o0, o1, o2, o3, *rest):
    width = 256
    depth = top.shape[0]
    if not final:
        held, sems = rest
        copies = fetches(bottom, depth, held, sems)
    hi, lo = split(v[...])
    pieces = jnp.concatenate([hi, lo], axis=0)
    for part, mat in enumerate((top, bottom if final else held)):
        if part == 1 and not final:
            for copy in copies:
                copy.wait()
        rows = slice(0, depth) if part == 0 else slice(depth, v.shape[1])
        for step in range(mat.shape[1] // width):
            at = slice(step * width, (step + 1) * width)
            both = dot(pieces[:, rows], mat[:, at], NN)
            both = both[:16] + both[16:]
            z[:, at] = both if part == 0 else z[:, at] + both
    for f, o in zip(faces_of(ints), (o0, o1, o2, o3)):
        pack_face(z, ints, f, o)
    if final:
        (dot_out,) = rest
        lane = lax.broadcasted_iota(jnp.int32, (16, BW), 1)
        dot_out[...] = place(lane, place_of(ints)[0], LOCAL, lane_sum(v[...] * z[...]))


def jumped_coupling(ints, both, i0, i1, i2, i3, b_hi, b_lo, full):
    y = place_of(ints)[0]
    full[...] = jnp.zeros_like(full)

    def rows(n):
        return pl.ds(pl.multiple_of(n * LANES, LANES), 24)

    full[rows(y), :] = both[16:40, :]
    beside = y + 2 * (y % 2) - 1
    places = (rows(4), rows(5), rows(y + 1 - 2 * (y % 2)), rows(jnp.clip(beside, 0, 3)))
    for f, to, got in zip(faces_of(ints), places, (i0, i1, i2, i3)):
        for c in range(4):
            b = ints[0, f * 4 + c]
            at = block_at(b)
            full[to, at] = jnp.where(b >= 0, -got[16:40, c * BW : (c + 1) * BW], full[to, at])
    hi, lo = split(full[...])
    b_hi[...] = hi
    b_lo[...] = lo


def unpacked_map(rows):
    slot = lax.broadcasted_iota(jnp.int32, rows[0].shape, 1) % LANES
    found = jnp.zeros_like(rows[0])
    for k, row in enumerate(rows):
        found = jnp.where(slot // PER == k, pltpu.roll(row, BW - (MAP - PER * k), 1), found)
    return found.astype(jnp.int32), slot


def picked_columns(pay, f_hi, f_lo, c_hi, c_lo):
    dofs = f_hi.shape[1]
    wanted = []
    for n in range(3):
        rows = [jnp.broadcast_to(pay[4 * n + k : 4 * n + k + 1, :], (8, BW)) for k in range(4)]
        wanted.append(unpacked_map(rows)[0][0:1, :])
    wanted = jnp.concatenate(wanted, axis=1)
    row = lax.broadcasted_iota(jnp.int32, (dofs, 3 * BW), 0)
    hot = (row == wanted).astype(F32).astype(BF16)
    c_hi[...] = dot(f_hi[...], hot, NN).astype(BF16)
    c_lo[...] = dot(f_lo[...], hot, NN).astype(BF16)


def coarse_half(first, t, near, *rest):
    if first:
        factor, out, f_hi, f_lo, top, hot, terms_at = rest
    else:
        f_hi, f_lo, top, hot, out, terms_at = rest
    groups = t.shape[0]
    owned = f_hi.shape[0]
    digits = f_hi.shape[1] // RADIX
    half = digits * 16
    if first:
        dof, slot = unpacked_map([t[:, k, :] for k in range(4)])
        top[...] = jnp.where(slot < 24, dof // RADIX, -1).astype(F32)
        low = (dof % RADIX).astype(F32)
        low = jnp.transpose(jnp.concatenate([low] * (BW // groups), axis=0))
        lane = lax.broadcasted_iota(jnp.int32, (BW, BW), 1).astype(F32)
        one, zero = (jnp.ones((BW, BW), BF16), jnp.zeros((BW, BW), BF16))
        for j in range(groups):
            column = jnp.broadcast_to(low[:, j : j + 1], (BW, BW)).astype(BF16)
            for n in range(RADIX // BW):
                wanted = (lane + float(n * BW)).astype(BF16)
                hot[j * BW : (j + 1) * BW, n * BW : (n + 1) * BW] = jnp.where(
                    wanted == column, one, zero
                )
    none = jnp.zeros((16, BW), BF16)

    def body(j, acc):
        terms = t[j]
        digit = jnp.broadcast_to(top[pl.ds(j, 1), :], (16, BW)).astype(BF16)
        hi, lo = split(terms)
        at = pl.ds(pl.multiple_of(j * BW, BW), BW)
        for d in range(digits):
            mine = digit == jnp.full((16, BW), d, BF16)
            terms_at[d * 16 : d * 16 + 16, at] = jnp.where(mine, hi, none)
            terms_at[half + d * 16 : half + d * 16 + 16, at] = jnp.where(mine, lo, none)
        return acc + terms

    total = lax.fori_loop(0, groups, body, jnp.zeros((16, BW), F32), unroll=4)
    sums = dot(terms_at[...], hot[...], NN)
    sums = sums[:half] + sums[half:]
    rhs = jnp.concatenate([sums[d * 16 : d * 16 + 16, :] for d in range(digits)], axis=1)
    hi, lo = split(rhs)
    pieces = jnp.concatenate([hi, lo], axis=0)
    if first:
        f_hi[...], f_lo[...] = split(factor[...])
    column = lax.broadcasted_iota(jnp.int32, (owned, 32), 1)
    mid = dot(f_hi[...], pieces, NT) + jnp.where(column < 16, dot(f_lo[...], pieces, NT), 0.0)
    mid = jnp.transpose(mid)
    out[:, 0:owned] = mid[:16] + mid[16:]
    out[:, owned : owned + BW] = total
    out[:, owned + BW :] = near[...]


def coarse_part(final, ints, own, got, face_one, face_two, c_hi, c_lo, part, out_one, out_two, scal):
    owned = c_hi.shape[0]
    mid = own[:, 0:owned] + got[:, 0:owned]
    total = own[:, owned : owned + BW] + got[:, owned : owned + BW]
    picked = dot3(mid, c_hi[...], c_lo[...], NN)
    lane = lax.broadcasted_iota(jnp.int32, (16, BW), 1)
    slot = lane % LANES

    def over(which):
        return lane_sum(jnp.where(which, total, 0.0))

    if final:
        energy = over(lane == place_of(ints)[0] * LANES + LOCAL) + lane_sum(mid * mid)
        wide = lax.broadcasted_iota(jnp.int32, picked.shape, 1)
        picked = jnp.where(wide == NORM, energy, picked)
        scal[...] = jnp.where(lane == 0, over(slot == CROSS), over(slot == SQUARE))
    else:
        scal[...] = jnp.broadcast_to(over(slot == NORM), (16, BW))
    width = picked.shape[1]
    part[...] = picked
    for out, beside in ((out_one, face_one), (out_two, face_two)):
        out[:, 0:width] = picked
        out[:, width:] = beside[...]


def jumped(out, z, ints, got, far, p0, p1, p2, p3, b_hi, b_lo):
    width = p0.shape[1]
    picked = (p0[...] + p1[:, 0:width]) + (p2[...] + p3[:, 0:width])
    y = place_of(ints)[0]
    lane = lax.broadcasted_iota(jnp.int32, (16, BW), 1)
    beside = pltpu.roll(picked[:, BW : 2 * BW], (BW - y * LANES) % BW, 1)
    beyond = pltpu.roll(picked[:, 2 * BW :], (BW + LANES - y * LANES) % BW, 1)
    beside = jnp.where(lane < LANES, beside, jnp.where(lane < 2 * LANES, beyond, 0.0))
    needed = jnp.concatenate([picked[:, 0:BW], beside], axis=1)
    out[...] = z[...] + dot3(needed, b_hi[...], b_lo[...], NN)
    near_at = got.shape[1] - 4 * BW
    subtract_faces(out, ints, ((got, near_at), (far, 0), (p1, width), (p3, width)))
    return picked


def next_vector(
    ints, z0, got, far, p0, p1, p2, p3, b_hi, b_lo, v0, bx_hi, bx_lo, weight, v1, pay
):
    jumped(v1, z0, ints, got, far, p0, p1, p2, p3, b_hi, b_lo)
    v = v1[...]
    w = v * weight[0:1, :]
    lane = lax.broadcasted_iota(jnp.int32, (16, BW), 1)
    y = place_of(ints)[0]
    pay[...] = (
        dot3(v, bx_hi[...], bx_lo[...], NT)
        + place(lane, y, CROSS, lane_sum(v0[...] * w))
        + place(lane, y, SQUARE, lane_sum(v * w))
    )


def finish(ints, z1, got, far, p0, p1, p2, p3, b_hi, b_lo, v0, v1, s0, s1, mult, resid):
    picked = jumped(resid, z1, ints, got, far, p0, p1, p2, p3, b_hi, b_lo)
    norm, cross, square = (s0[:, 0:1], s1[:, 0:1], s1[:, 1:2])
    energy = picked[:, NORM : NORM + 1]
    step1 = norm / cross
    fresh = norm - 2.0 * step1 * cross + step1 * step1 * square
    c = 1.0 + fresh / norm
    curvature = c * c * cross - 2.0 * c * step1 * square + step1 * step1 * energy
    step2 = fresh / curvature
    first, second = (v0[...], v1[...])
    mult[...] = (step1 + step2 * c) * first - (step2 * step1) * second
    resid[...] = first - (step1 + step2 * c) * second + (step2 * step1) * resid[...]


def call(kernel, name, ins, outs, scalars, micros, scratch=(), mib=8, outside=()):
    specs = [SMEM] * scalars + [VMEM] * (len(ins) - scalars)
    for n in outside:
        specs[n] = pl.BlockSpec(memory_space=pl.ANY)
    return pl.pallas_call(
        kernel,
        out_shape=[jax.ShapeDtypeStruct(s, d) for s, d in outs],
        in_specs=specs,
        out_specs=[VMEM] * len(outs),
        scratch_shapes=[pltpu.VMEM(*s) if isinstance(s, tuple) else s for s in scratch],
        compiler_params=pltpu.CompilerParams(vmem_limit_bytes=mib * 1024 * 1024),
        cost_estimate=pl.CostEstimate(
            flops=int(micros * 1e6), bytes_accessed=int(micros * 3.5e6), transcendentals=0
        ),
        name=name,
    )(*ins)


def per_device(interface_load, flexibility, corner_coupling, coarse_factor, face_slots, corner_map):
    both = jnp.concatenate([interface_load[0], corner_coupling[0]], axis=0)
    cases, dofs = interface_load.shape[1:]
    owned, coarse_dofs = coarse_factor.shape
    zs, xs, cs, ys = (lax.axis_size(a) for a in ALL)
    subs = zs * xs * cs
    face = 4 * BW
    ahead = dofs * 7 // 8
    here = jnp.stack([lax.axis_index("y"), lax.axis_index("c")]).astype(jnp.int32)
    wide = corner_map.shape[1]
    table = jnp.concatenate(
        [
            jnp.pad(face_slots[0], ((0, 0), (0, wide - face_slots.shape[2]))),
            corner_map,
            jnp.pad(here[None], ((0, 0), (0, wide - 2))),
        ]
    )
    near_pairs = [(i, i ^ 1) for i in range(cs)]
    far_pairs = [(i, (i + 1) % subs) for i in range(1, subs, 2)]
    far_pairs = far_pairs + [(j, i) for i, j in far_pairs]
    one_pairs = [(j, j ^ 1) for j in range(ys)]
    across_pairs = [(j, j ^ 2) for j in range(ys)]
    two_pairs = [(j, j ^ 3) for j in range(ys)]

    def near(p):
        return lax.ppermute(p, "c", near_pairs)

    def far(p):
        return lax.ppermute(p, SUB, far_pairs)

    def one(p):
        return lax.ppermute(p, "y", one_pairs)

    def across(p):
        return lax.ppermute(p, "y", across_pairs)

    def two(p):
        return lax.ppermute(p, "y", two_pairs)

    def gather(row):
        every = jnp.broadcast_to(row[None], (zs * xs,) + row.shape)
        return lax.all_to_all(every, ("z", "x"), 0, 0)

    def product(final, v):
        outs = [((cases, dofs), F32)] + [((cases, face), F32)] * 4
        outs = outs + [((cases, BW), F32) if final else ((dofs - ahead, dofs), BF16)]
        return call(
            functools.partial(local_product, final),
            "local_product",
            (ints, v, top, bottom if final else flexibility[0]),
            outs,
            1,
            2,
            () if final else (pltpu.SemaphoreType.DMA((CHUNKS,)),),
            mib=6 if final else FETCH,
            outside=() if final else (3,),
        )

    def half(first, t, face_near, *held):
        terms = t.shape[0] * BW
        outs = [((cases, owned + BW + face), F32)]
        if first:
            outs = outs + [((owned, coarse_dofs), BF16)] * 2
            outs = outs + [((t.shape[0], BW), F32), ((terms, RADIX), BF16)]
        return call(
            functools.partial(coarse_half, first),
            "coarse_half",
            (t, face_near, *held),
            outs,
            0,
            4,
            [((2 * cases * (coarse_dofs // RADIX), terms), BF16)],
            mib=16,
        )

    def rest_of_solve(final, own, face_one, face_two):
        got = near(own)
        wide = 3 * BW
        part, out_one, out_two, scal = call(
            functools.partial(coarse_part, final),
            "coarse_part",
            (ints, own, got, face_one, face_two, c_hi, c_lo),
            [((cases, wide), F32)] + [((cases, wide + face), F32)] * 2 + [((cases, BW), F32)],
            1,
            1,
        )
        return scal, got, part, one(out_one), across(part), two(out_two)

    o0, o1, o2, o3, own_map, ints = call(
        first_pack,
        "first_pack",
        (table, both),
        [((48, face), F32)] * 2
        + [((40, face), F32)] * 2
        + [((8, BW), F32), ((1, BW), jnp.int32)],
        1,
        1,
    )
    far_came = far(o1)
    came = (near(o0), far_came, one(o2), two(o3))
    bx_hi, bx_lo, weight, top = call(
        spread_coupling,
        "spread_coupling",
        (ints, both, flexibility[0]),
        [((BW, dofs), BF16)] * 2 + [((8, dofs), F32), ((ahead, dofs), BF16)],
        1,
        3,
        [((BW, dofs), F32), pltpu.SemaphoreType.DMA((CHUNKS,))],
        mib=FETCH,
        outside=(2,),
    )
    v0, pay = call(
        first_vector,
        "first_vector",
        (ints, both, *came, bx_hi, bx_lo, weight, own_map),
        [((cases, dofs), F32), ((cases, BW), F32)],
        1,
        1,
    )
    rows = (two(pay), one(pay), across(pay))
    *rows, z0, n0, f0, a0, b0, bottom = lax.optimization_barrier((*rows, *product(False, v0)))
    faces = (n0, f0, a0, b0)
    row = (pay + rows[0]) + (rows[1] + rows[2])
    terms0, face_far = lax.optimization_barrier((gather(row), faces[1]))
    face_far = far(face_far)
    own, *held = half(True, terms0, faces[0], coarse_factor)
    f_hi, f_lo = held[:2]
    c_hi, c_lo = call(
        picked_columns,
        "picked_columns",
        (row, f_hi, f_lo),
        [((owned, 3 * BW), BF16)] * 2,
        0,
        2.5,
        mib=16,
    )
    b_hi, b_lo = call(
        jumped_coupling,
        "jumped_coupling",
        (ints, both, *came),
        [((2 * BW, dofs), BF16)] * 2,
        1,
        1.2,
        [((2 * BW, dofs), F32)],
        mib=10,
    )
    scal0, got, *parts = rest_of_solve(False, own, faces[2], faces[3])
    v1, pay = call(
        next_vector,
        "next_vector",
        (ints, z0, got, face_far, *parts, b_hi, b_lo, v0, bx_hi, bx_lo, weight),
        [((cases, dofs), F32), ((cases, BW), F32)],
        1,
        1.6,
        mib=12,
    )
    rows = (two(pay), one(pay), across(pay))
    *rows, z1, n1, f1, a1, b1, local_dot = lax.optimization_barrier((*rows, *product(True, v1)))
    faces = (n1, f1, a1, b1)
    row = (pay + rows[0]) + (rows[1] + rows[2]) + local_dot
    terms1, face_far = lax.optimization_barrier((gather(row), faces[1]))
    face_far = far(face_far)
    (own,) = half(False, terms1, faces[0], *held)
    scal1, got, *parts = rest_of_solve(True, own, faces[2], faces[3])
    mult, resid = call(
        finish,
        "finish",
        (ints, z1, got, face_far, *parts, b_hi, b_lo, v0, v1, scal0, scal1),
        [((cases, dofs), F32)] * 2,
        1,
        1.9,
        mib=12,
    )
    return mult[None], resid[None]


def solution(mesh):
    fine = Mesh(mesh.devices.reshape(8, 4, 2, 4), ALL)
    in_specs = (
        P(ALL, None, None),
        P(ALL, None, None),
        P(ALL, None, None),
        P("y", None),
        P(ALL, None, None),
        P(ALL, None),
    )
    out_specs = (P(ALL, None, None), P(ALL, None, None))
    return jax.shard_map(
        per_device, mesh=fine, in_specs=in_specs, out_specs=out_specs, check_vma=False
    )
```

```python
import functools

import jax
import jax.numpy as jnp
from jax import lax
from jax.experimental import pallas as pl
from jax.experimental.pallas import tpu as pltpu
from jax.sharding import Mesh, PartitionSpec as P

BW = 128
LANES = 32
NORM, CROSS, SQUARE, LOCAL = 24, 25, 26, 27
MAP, PER = 26, 6
RADIX = 256
F32, BF16 = jnp.float32, jnp.bfloat16
ALL = ("z", "x", "c", "y")
SUB = ("z", "x", "c")
FETCH = 44
CHUNKS = 8

NN = (((1,), (0,)), ((), ()))
NT = (((1,), (1,)), ((), ()))

VMEM = pl.BlockSpec(memory_space=pltpu.VMEM)
SMEM = pl.BlockSpec(memory_space=pltpu.SMEM)


def split(x):
    hi = x.astype(BF16)
    return hi, (x - hi.astype(F32)).astype(BF16)


def dot(a, b, dims):
    return lax.dot_general(a, b, dims, preferred_element_type=F32)


def dot3(a, b_hi, b_lo, dims):
    rows = a.shape[0]
    a_hi, a_lo = split(a)
    both = dot(jnp.concatenate([a_hi, a_lo], axis=0), b_hi, dims)
    return both[:rows] + both[rows:] + dot(a_hi, b_lo, dims)


def block_at(b):
    return pl.ds(pl.multiple_of(jnp.maximum(b, 0) * BW, BW), BW)


def place_of(ints):
    return ints[0, 40], ints[0, 41]


def faces_of(ints):
    y, core = place_of(ints)
    odd = y % 2
    return (1 - core, core, 3 - odd, 2 + odd)


def subtract_faces(ref, ints, incoming):
    for f, (got, col0) in zip(faces_of(ints), incoming):
        for c in range(4):
            b = ints[0, f * 4 + c]
            at = block_at(b)
            held = ref[:, at]
            ref[:, at] = jnp.where(b >= 0, held - got[0:16, col0 + c * BW : col0 + (c + 1) * BW], held)


def pack_face(values, ints, f, out):
    rows = values.shape[0]
    for c in range(4):
        out[0:rows, c * BW : (c + 1) * BW] = values[:, block_at(ints[0, f * 4 + c])]


def lane_sum(x):
    return jnp.sum(x, axis=1, keepdims=True)


def place(lane, y, slot, column):
    return jnp.where(lane == y * LANES + slot, column, 0.0)


def first_pack(table, both, o0, o1, o2, o3, own_map, ints):
    flat = [table[f, c] for f in range(4) for c in range(4)]
    flat = flat + [table[4, j] for j in range(24)] + [table[5, 0], table[5, 1]]
    row = lax.broadcasted_iota(jnp.int32, (8, BW), 0)
    at = lax.broadcasted_iota(jnp.int32, (8, BW), 1)
    every = jnp.zeros((8, BW), jnp.int32)
    for n, value in enumerate(flat):
        every = jnp.where(at == n, value, every)
    ints[...] = every[0:1, :]
    y, core = (flat[40], flat[41])
    lane = at - (y * LANES + MAP)
    placed = jnp.zeros((8, BW), jnp.int32)
    for j in range(24):
        here = jnp.logical_and(row == j // PER, lane == j % PER)
        placed = jnp.where(here, flat[16 + j], placed)
    placed = placed.astype(F32)
    own_map[...] = placed
    for f, o in zip((1 - core, core, 3 - y % 2, 2 + y % 2), (o0, o1, o2, o3)):
        for c in range(4):
            o[0:40, c * BW : (c + 1) * BW] = both[:, block_at(table[f, c])]
    for o in (o0, o1):
        o[40:48, 0:BW] = placed
        o[40:48, BW:] = jnp.zeros((8, 3 * BW), F32)


def fetches(mat, row0, held, sems):
    rows = held.shape[0] // CHUNKS
    copies = []
    for n in range(CHUNKS):
        copies.append(
            pltpu.make_async_copy(
                mat.at[pl.ds(row0 + n * rows, rows)], held.at[pl.ds(n * rows, rows)], sems.at[n]
            )
        )
        copies[n].start()
    return copies


def spread_coupling(ints, both, mat, bx_hi, bx_lo, weight, held, bx, sems):
    copies = fetches(mat, 0, held, sems)
    bx[...] = jnp.zeros_like(bx)
    bx[pl.ds(pl.multiple_of(place_of(ints)[0] * LANES, LANES), 24), :] = both[16:40, :]
    hi, lo = split(bx[...])
    bx_hi[...] = hi
    bx_lo[...] = lo
    weight[...] = jnp.ones_like(weight)
    for f in range(4):
        for c in range(4):
            b = ints[0, f * 4 + c]
            at = block_at(b)
            weight[:, at] = jnp.where(b >= 0, jnp.full((8, BW), 0.5, F32), weight[:, at])
    for copy in copies:
        copy.wait()


def first_vector(ints, both, i0, i1, i2, i3, bx_hi, bx_lo, weight, own_map, v0, pay):
    v0[...] = both[0:16, :]
    subtract_faces(v0, ints, [(i, 0) for i in (i0, i1, i2, i3)])
    v = v0[...]
    norm = lane_sum(v * v * weight[0:1, :])
    lane = lax.broadcasted_iota(jnp.int32, (16, BW), 1)
    maps = jnp.concatenate(
        [own_map[0:4, :], i0[40:44, 0:BW], i1[40:44, 0:BW], jnp.zeros((4, BW), F32)], axis=0
    )
    pay[...] = dot3(v, bx_hi[...], bx_lo[...], NT) + place(lane, place_of(ints)[0], NORM, norm) + maps


def local_product(final, ints, v, top, bottom, z, o0, o1, o2, o3, *rest):
    width = 256
    depth = top.shape[0]
    if not final:
        held, sems = rest
        copies = fetches(bottom, depth, held, sems)
    hi, lo = split(v[...])
    pieces = jnp.concatenate([hi, lo], axis=0)
    for part, mat in enumerate((top, bottom if final else held)):
        if part == 1 and not final:
            for copy in copies:
                copy.wait()
        rows = slice(0, depth) if part == 0 else slice(depth, v.shape[1])
        for step in range(mat.shape[1] // width):
            at = slice(step * width, (step + 1) * width)
            both = dot(pieces[:, rows], mat[:, at], NN)
            both = both[:16] + both[16:]
            z[:, at] = both if part == 0 else z[:, at] + both
    for f, o in zip(faces_of(ints), (o0, o1, o2, o3)):
        pack_face(z, ints, f, o)
    if final:
        (dot_out,) = rest
        lane = lax.broadcasted_iota(jnp.int32, (16, BW), 1)
        dot_out[...] = place(lane, place_of(ints)[0], LOCAL, lane_sum(v[...] * z[...]))


def jumped_coupling(ints, both, i0, i1, i2, i3, b_hi, b_lo, full):
    y = place_of(ints)[0]
    full[...] = jnp.zeros_like(full)

    def rows(n):
        return pl.ds(pl.multiple_of(n * LANES, LANES), 24)

    full[rows(y), :] = both[16:40, :]
    beside = y + 2 * (y % 2) - 1
    places = (rows(4), rows(5), rows(y + 1 - 2 * (y % 2)), rows(jnp.clip(beside, 0, 3)))
    for f, to, got in zip(faces_of(ints), places, (i0, i1, i2, i3)):
        for c in range(4):
            b = ints[0, f * 4 + c]
            at = block_at(b)
            full[to, at] = jnp.where(b >= 0, -got[16:40, c * BW : (c + 1) * BW], full[to, at])
    hi, lo = split(full[...])
    b_hi[...] = hi
    b_lo[...] = lo


def unpacked_map(rows):
    slot = lax.broadcasted_iota(jnp.int32, rows[0].shape, 1) % LANES
    found = jnp.zeros_like(rows[0])
    for k, row in enumerate(rows):
        found = jnp.where(slot // PER == k, pltpu.roll(row, BW - (MAP - PER * k), 1), found)
    return found.astype(jnp.int32), slot


def picked_columns(pay, f_hi, f_lo, c_hi, c_lo):
    dofs = f_hi.shape[1]
    wanted = []
    for n in range(3):
        rows = [jnp.broadcast_to(pay[4 * n + k : 4 * n + k + 1, :], (8, BW)) for k in range(4)]
        wanted.append(unpacked_map(rows)[0][0:1, :])
    wanted = jnp.concatenate(wanted, axis=1)
    row = lax.broadcasted_iota(jnp.int32, (dofs, 3 * BW), 0)
    hot = (row == wanted).astype(F32).astype(BF16)
    c_hi[...] = dot(f_hi[...], hot, NN).astype(BF16)
    c_lo[...] = dot(f_lo[...], hot, NN).astype(BF16)


def coarse_half(first, t, near, *rest):
    if first:
        factor, out, f_hi, f_lo, top, hot, terms_at = rest
    else:
        f_hi, f_lo, top, hot, out, terms_at = rest
    groups = t.shape[0]
    owned = f_hi.shape[0]
    digits = f_hi.shape[1] // RADIX
    half = digits * 16
    if first:
        dof, slot = unpacked_map([t[:, k, :] for k in range(4)])
        top[...] = jnp.where(slot < 24, dof // RADIX, -1).astype(F32)
        low = (dof % RADIX).astype(F32)
        low = jnp.transpose(jnp.concatenate([low] * (BW // groups), axis=0))
        lane = lax.broadcasted_iota(jnp.int32, (BW, BW), 1).astype(F32)
        one, zero = (jnp.ones((BW, BW), BF16), jnp.zeros((BW, BW), BF16))
        for j in range(groups):
            column = jnp.broadcast_to(low[:, j : j + 1], (BW, BW)).astype(BF16)
            for n in range(RADIX // BW):
                wanted = (lane + float(n * BW)).astype(BF16)
                hot[j * BW : (j + 1) * BW, n * BW : (n + 1) * BW] = jnp.where(
                    wanted == column, one, zero
                )
    none = jnp.zeros((16, BW), BF16)

    total = jnp.zeros((16, BW), F32)
    for j in range(groups):
        terms = t[j]
        digit = jnp.broadcast_to(top[j : j + 1, :], (16, BW)).astype(BF16)
        hi, lo = split(terms)
        at = slice(j * BW, (j + 1) * BW)
        for d in range(digits):
            mine = digit == jnp.full((16, BW), d, BF16)
            terms_at[d * 16 : d * 16 + 16, at] = jnp.where(mine, hi, none)
            terms_at[half + d * 16 : half + d * 16 + 16, at] = jnp.where(mine, lo, none)
        total = total + terms
    sums = dot(terms_at[...], hot[...], NN)
    sums = sums[:half] + sums[half:]
    rhs = jnp.concatenate([sums[d * 16 : d * 16 + 16, :] for d in range(digits)], axis=1)
    hi, lo = split(rhs)
    pieces = jnp.concatenate([hi, lo], axis=0)
    if first:
        f_hi[...], f_lo[...] = split(factor[...])
    column = lax.broadcasted_iota(jnp.int32, (owned, 32), 1)
    mid = dot(f_hi[...], pieces, NT) + jnp.where(column < 16, dot(f_lo[...], pieces, NT), 0.0)
    mid = jnp.transpose(mid)
    out[:, 0:owned] = mid[:16] + mid[16:]
    out[:, owned : owned + BW] = total
    out[:, owned + BW :] = near[...]


def coarse_part(final, ints, own, got, face_one, face_two, c_hi, c_lo, part, out_one, out_two, scal):
    owned = c_hi.shape[0]
    mid = own[:, 0:owned] + got[:, 0:owned]
    total = own[:, owned : owned + BW] + got[:, owned : owned + BW]
    picked = dot3(mid, c_hi[...], c_lo[...], NN)
    lane = lax.broadcasted_iota(jnp.int32, (16, BW), 1)
    slot = lane % LANES

    def over(which):
        return lane_sum(jnp.where(which, total, 0.0))

    if final:
        energy = over(lane == place_of(ints)[0] * LANES + LOCAL) + lane_sum(mid * mid)
        wide = lax.broadcasted_iota(jnp.int32, picked.shape, 1)
        picked = jnp.where(wide == NORM, energy, picked)
        scal[...] = jnp.where(lane == 0, over(slot == CROSS), over(slot == SQUARE))
    else:
        scal[...] = jnp.broadcast_to(over(slot == NORM), (16, BW))
    width = picked.shape[1]
    part[...] = picked
    for out, beside in ((out_one, face_one), (out_two, face_two)):
        out[:, 0:width] = picked
        out[:, width:] = beside[...]


def jumped(out, z, ints, got, far, p0, p1, p2, p3, b_hi, b_lo):
    width = p0.shape[1]
    picked = (p0[...] + p1[:, 0:width]) + (p2[...] + p3[:, 0:width])
    y = place_of(ints)[0]
    lane = lax.broadcasted_iota(jnp.int32, (16, BW), 1)
    beside = pltpu.roll(picked[:, BW : 2 * BW], (BW - y * LANES) % BW, 1)
    beyond = pltpu.roll(picked[:, 2 * BW :], (BW + LANES - y * LANES) % BW, 1)
    beside = jnp.where(lane < LANES, beside, jnp.where(lane < 2 * LANES, beyond, 0.0))
    needed = jnp.concatenate([picked[:, 0:BW], beside], axis=1)
    out[...] = z[...] + dot3(needed, b_hi[...], b_lo[...], NN)
    near_at = got.shape[1] - 4 * BW
    subtract_faces(out, ints, ((got, near_at), (far, 0), (p1, width), (p3, width)))
    return picked


def next_vector(
    ints, z0, got, far, p0, p1, p2, p3, b_hi, b_lo, v0, bx_hi, bx_lo, weight, v1, pay
):
    jumped(v1, z0, ints, got, far, p0, p1, p2, p3, b_hi, b_lo)
    v = v1[...]
    w = v * weight[0:1, :]
    lane = lax.broadcasted_iota(jnp.int32, (16, BW), 1)
    y = place_of(ints)[0]
    pay[...] = (
        dot3(v, bx_hi[...], bx_lo[...], NT)
        + place(lane, y, CROSS, lane_sum(v0[...] * w))
        + place(lane, y, SQUARE, lane_sum(v * w))
    )


def finish(ints, z1, got, far, p0, p1, p2, p3, b_hi, b_lo, v0, v1, s0, s1, mult, resid):
    picked = jumped(resid, z1, ints, got, far, p0, p1, p2, p3, b_hi, b_lo)
    norm, cross, square = (s0[:, 0:1], s1[:, 0:1], s1[:, 1:2])
    energy = picked[:, NORM : NORM + 1]
    step1 = norm / cross
    fresh = norm - 2.0 * step1 * cross + step1 * step1 * square
    c = 1.0 + fresh / norm
    curvature = c * c * cross - 2.0 * c * step1 * square + step1 * step1 * energy
    step2 = fresh / curvature
    first, second = (v0[...], v1[...])
    mult[...] = (step1 + step2 * c) * first - (step2 * step1) * second
    resid[...] = first - (step1 + step2 * c) * second + (step2 * step1) * resid[...]


def call(kernel, name, ins, outs, scalars, micros, scratch=(), mib=8, outside=()):
    specs = [SMEM] * scalars + [VMEM] * (len(ins) - scalars)
    for n in outside:
        specs[n] = pl.BlockSpec(memory_space=pl.ANY)
    return pl.pallas_call(
        kernel,
        out_shape=[jax.ShapeDtypeStruct(s, d) for s, d in outs],
        in_specs=specs,
        out_specs=[VMEM] * len(outs),
        scratch_shapes=[pltpu.VMEM(*s) if isinstance(s, tuple) else s for s in scratch],
        compiler_params=pltpu.CompilerParams(vmem_limit_bytes=mib * 1024 * 1024),
        cost_estimate=pl.CostEstimate(
            flops=int(micros * 1e6), bytes_accessed=int(micros * 3.5e6), transcendentals=0
        ),
        name=name,
    )(*ins)


def per_device(interface_load, flexibility, corner_coupling, coarse_factor, face_slots, corner_map):
    both = jnp.concatenate([interface_load[0], corner_coupling[0]], axis=0)
    cases, dofs = interface_load.shape[1:]
    owned, coarse_dofs = coarse_factor.shape
    zs, xs, cs, ys = (lax.axis_size(a) for a in ALL)
    subs = zs * xs * cs
    face = 4 * BW
    ahead = dofs * 7 // 8
    here = jnp.stack([lax.axis_index("y"), lax.axis_index("c")]).astype(jnp.int32)
    wide = corner_map.shape[1]
    table = jnp.concatenate(
        [
            jnp.pad(face_slots[0], ((0, 0), (0, wide - face_slots.shape[2]))),
            corner_map,
            jnp.pad(here[None], ((0, 0), (0, wide - 2))),
        ]
    )
    near_pairs = [(i, i ^ 1) for i in range(cs)]
    far_pairs = [(i, (i + 1) % subs) for i in range(1, subs, 2)]
    far_pairs = far_pairs + [(j, i) for i, j in far_pairs]
    one_pairs = [(j, j ^ 1) for j in range(ys)]
    across_pairs = [(j, j ^ 2) for j in range(ys)]
    two_pairs = [(j, j ^ 3) for j in range(ys)]

    def near(p):
        return lax.ppermute(p, "c", near_pairs)

    def far(p):
        return lax.ppermute(p, SUB, far_pairs)

    def one(p):
        return lax.ppermute(p, "y", one_pairs)

    def across(p):
        return lax.ppermute(p, "y", across_pairs)

    def two(p):
        return lax.ppermute(p, "y", two_pairs)

    def gather(row):
        every = jnp.broadcast_to(row[None], (zs * xs,) + row.shape)
        return lax.all_to_all(every, ("z", "x"), 0, 0)

    def product(final, v):
        outs = [((cases, dofs), F32)] + [((cases, face), F32)] * 4
        outs = outs + [((cases, BW), F32) if final else ((dofs - ahead, dofs), BF16)]
        return call(
            functools.partial(local_product, final),
            "local_product",
            (ints, v, top, bottom if final else flexibility[0]),
            outs,
            1,
            2,
            () if final else (pltpu.SemaphoreType.DMA((CHUNKS,)),),
            mib=6 if final else FETCH,
            outside=() if final else (3,),
        )

    def half(first, t, face_near, *held):
        terms = t.shape[0] * BW
        outs = [((cases, owned + BW + face), F32)]
        if first:
            outs = outs + [((owned, coarse_dofs), BF16)] * 2
            outs = outs + [((t.shape[0], BW), F32), ((terms, RADIX), BF16)]
        return call(
            functools.partial(coarse_half, first),
            "coarse_half",
            (t, face_near, *held),
            outs,
            0,
            4,
            [((2 * cases * (coarse_dofs // RADIX), terms), BF16)],
            mib=16,
        )

    def rest_of_solve(final, own, face_one, face_two):
        got = near(own)
        wide = 3 * BW
        part, out_one, out_two, scal = call(
            functools.partial(coarse_part, final),
            "coarse_part",
            (ints, own, got, face_one, face_two, c_hi, c_lo),
            [((cases, wide), F32)] + [((cases, wide + face), F32)] * 2 + [((cases, BW), F32)],
            1,
            1,
        )
        return scal, got, part, one(out_one), across(part), two(out_two)

    o0, o1, o2, o3, own_map, ints = call(
        first_pack,
        "first_pack",
        (table, both),
        [((48, face), F32)] * 2
        + [((40, face), F32)] * 2
        + [((8, BW), F32), ((1, BW), jnp.int32)],
        1,
        1,
    )
    far_came = far(o1)
    came = (near(o0), far_came, one(o2), two(o3))
    bx_hi, bx_lo, weight, top = call(
        spread_coupling,
        "spread_coupling",
        (ints, both, flexibility[0]),
        [((BW, dofs), BF16)] * 2 + [((8, dofs), F32), ((ahead, dofs), BF16)],
        1,
        3,
        [((BW, dofs), F32), pltpu.SemaphoreType.DMA((CHUNKS,))],
        mib=FETCH,
        outside=(2,),
    )
    v0, pay = call(
        first_vector,
        "first_vector",
        (ints, both, *came, bx_hi, bx_lo, weight, own_map),
        [((cases, dofs), F32), ((cases, BW), F32)],
        1,
        1,
    )
    rows = (two(pay), one(pay), across(pay))
    *rows, z0, n0, f0, a0, b0, bottom = lax.optimization_barrier((*rows, *product(False, v0)))
    faces = (n0, f0, a0, b0)
    row = (pay + rows[0]) + (rows[1] + rows[2])
    terms0, face_far = lax.optimization_barrier((gather(row), faces[1]))
    face_far = far(face_far)
    own, *held = half(True, terms0, faces[0], coarse_factor)
    f_hi, f_lo = held[:2]
    c_hi, c_lo = call(
        picked_columns,
        "picked_columns",
        (row, f_hi, f_lo),
        [((owned, 3 * BW), BF16)] * 2,
        0,
        2.5,
        mib=16,
    )
    b_hi, b_lo = call(
        jumped_coupling,
        "jumped_coupling",
        (ints, both, *came),
        [((2 * BW, dofs), BF16)] * 2,
        1,
        1.2,
        [((2 * BW, dofs), F32)],
        mib=10,
    )
    scal0, got, *parts = rest_of_solve(False, own, faces[2], faces[3])
    v1, pay = call(
        next_vector,
        "next_vector",
        (ints, z0, got, face_far, *parts, b_hi, b_lo, v0, bx_hi, bx_lo, weight),
        [((cases, dofs), F32), ((cases, BW), F32)],
        1,
        1.6,
        mib=12,
    )
    rows = (two(pay), one(pay), across(pay))
    *rows, z1, n1, f1, a1, b1, local_dot = lax.optimization_barrier((*rows, *product(True, v1)))
    faces = (n1, f1, a1, b1)
    row = (pay + rows[0]) + (rows[1] + rows[2]) + local_dot
    terms1, face_far = lax.optimization_barrier((gather(row), faces[1]))
    face_far = far(face_far)
    (own,) = half(False, terms1, faces[0], *held)
    scal1, got, *parts = rest_of_solve(True, own, faces[2], faces[3])
    mult, resid = call(
        finish,
        "finish",
        (ints, z1, got, face_far, *parts, b_hi, b_lo, v0, v1, scal0, scal1),
        [((cases, dofs), F32)] * 2,
        1,
        1.9,
        mib=12,
    )
    return mult[None], resid[None]


def solution(mesh):
    fine = Mesh(mesh.devices.reshape(8, 4, 2, 4), ALL)
    in_specs = (
        P(ALL, None, None),
        P(ALL, None, None),
        P(ALL, None, None),
        P("y", None),
        P(ALL, None, None),
        P(ALL, None),
    )
    out_specs = (P(ALL, None, None), P(ALL, None, None))
    return jax.shard_map(
        per_device, mesh=fine, in_specs=in_specs, out_specs=out_specs, check_vma=False
    )
```
